32 devices in a mesh: blk: 4 (over y, x), grp: 8 (over z, core).
Axes of the slice: x: 2, y: 2, z: 4, core: 2. Of those that a mesh axis runs over, the one named last changes fastest.
Arguments:
- queries: bfloat16 [8, 128, 1280], P('blk'), may hold values from -8 to 8
- query_lengths: int32 [8], P('blk'), may hold values from 32 to 128, as said below
- targets: bfloat16 [128, 128, 1280], P(('blk', 'grp')), may hold values from -8 to 8
- target_lengths: int32 [128], P(('blk', 'grp')), may hold values from 32 to 128, as said below
Outputs:
- profile: float32 [8, 128, 1280], P('blk', 'grp')
- similarity: float32 [8, 128], P('blk', 'grp')
The draws below stay inside these ranges and needn't reach their ends.
Inputs may be any that keep to these rules, and one draw needn't show every extreme that they name: The first query_lengths[q] residues of query q are valid, the rest is padding; some query has all 128. The first target_lengths[t] residues of target t are valid, the rest is padding; some target has all 128.
All inputs are finite; a program needn't handle non-finite values.
Results may differ from the reference program's by a relative error of at most 0.00079.
Values may be sent and summed in bfloat16 or wider, within the bound.
A program may use at most 64 MiB of HBM per device.

```python
import math
import jax
import jax.numpy as jnp
from jax import lax

D = 1280
L = 128
QDEV = 2
TB = 4
STEPS = 3
NQ = 8
NT = 128
N_BLK = 4
N_GRP = 8


def base_values(key, shape):
    return jnp.clip(jax.random.normal(key, shape, jnp.float32), -6.0, 6.0)


def draw_queries(key, part):
    values = base_values(jax.random.fold_in(key, 1), (NQ, L, D))
    return jnp.clip(values, -8.0, 8.0).astype(jnp.bfloat16)


def draw_targets(key, part):
    values = base_values(jax.random.fold_in(key, 3), (NT, L, D))
    return jnp.clip(values, -8.0, 8.0).astype(jnp.bfloat16)


def draw_query_lengths(key, part):
    drawn = jax.random.randint(jax.random.fold_in(key, 11), (NQ,), L // 4, L + 1, jnp.int32)
    chosen = jax.random.randint(jax.random.fold_in(key, 12), (), 0, NQ, jnp.int32)
    return drawn.at[chosen].set(L)


def draw_target_lengths(key, part):
    drawn = jax.random.randint(jax.random.fold_in(key, 13), (NT,), L // 4, L + 1, jnp.int32)
    chosen = jax.random.randint(jax.random.fold_in(key, 14), (), 0, NT, jnp.int32)
    return drawn.at[chosen].set(L)


def setup_inputs(seed: int = 0) -> dict:
    splits = jax.random.split(jax.random.key(seed), 5)
    return {
        "queries": draw_queries(jax.random.fold_in(splits[4], 71), 0),
        "query_lengths": draw_query_lengths(jax.random.fold_in(splits[4], 71), 0),
        "targets": draw_targets(jax.random.fold_in(splits[4], 71), 0),
        "target_lengths": draw_target_lengths(jax.random.fold_in(splits[4], 71), 0),
    }


def align_pair(query_rows, query_len, target_rows, target_len):
    scale = 3.0 / math.sqrt(query_rows.shape[-1])
    scores = jnp.einsum('qid,mjd->qmij', query_rows.astype(jnp.float32), target_rows.astype(jnp.float32)) * scale
    positions = jnp.arange(query_rows.shape[1], dtype=jnp.int32)
    row_ok = positions[None, :] < query_len[:, None]
    col_ok = positions[None, :] < target_len[:, None]
    row_mask = row_ok[:, None, :, None]
    col_mask = col_ok[None, :, None, :]
    row_top = lax.optimization_barrier(jnp.max(jnp.where(col_mask, scores, -jnp.inf), axis=3, keepdims=True))
    row_exp = jnp.where(col_mask, jnp.exp(scores - row_top), 0.0)
    row_soft = jnp.where(row_mask, row_exp / lax.optimization_barrier(jnp.sum(row_exp, axis=3, keepdims=True)), 0.0)
    col_top = lax.optimization_barrier(jnp.max(jnp.where(row_mask, scores, -jnp.inf), axis=2, keepdims=True))
    col_exp = jnp.where(row_mask, jnp.exp(scores - col_top), 0.0)
    col_soft = jnp.where(col_mask, col_exp / lax.optimization_barrier(jnp.sum(col_exp, axis=2, keepdims=True)), 0.0)
    weights = row_soft + col_soft - row_soft * col_soft
    similarity = lax.optimization_barrier(jnp.sum(weights * scores, axis=(2, 3))) / lax.optimization_barrier(jnp.sum(weights, axis=(2, 3)))
    rounded = lax.optimization_barrier(row_soft.astype(jnp.bfloat16))
    profile = jnp.einsum('qmij,mjd->qid', rounded.astype(jnp.float32), target_rows.astype(jnp.float32))
    return (similarity, profile)

def reference(queries, query_lengths, targets, target_lengths):
    query_sets = queries.reshape(N_BLK, QDEV, L, D)
    query_lens = query_lengths.reshape(N_BLK, QDEV)
    target_sets = targets.reshape(N_BLK, N_GRP * TB, L, D)
    target_lens = target_lengths.reshape(N_BLK, N_GRP * TB)
    profile_scale = 1.0 / math.sqrt(N_GRP * TB * (STEPS + 1))

    def one_set(inputs):
        cycle_index, query_rows, query_len = inputs
        running = jnp.zeros((QDEV, L, D), jnp.float32)
        gathered = []
        for offset in range(STEPS + 1):
            source = ((cycle_index - offset) % N_BLK).astype(jnp.int32)
            target_rows = lax.dynamic_index_in_dim(target_sets, source, 0, keepdims=False)
            target_len = lax.dynamic_index_in_dim(target_lens, source, 0, keepdims=False)
            pair_sim, pair_prof = align_pair(query_rows, query_len, target_rows, target_len)
            running = running + pair_prof
            gathered.append(pair_sim.reshape(QDEV, N_GRP, TB))
        similarity = jnp.stack(gathered, axis=2).reshape(QDEV, N_GRP * (STEPS + 1) * TB)
        return (running * profile_scale, similarity)
    profile, similarity = lax.map(one_set, (jnp.arange(N_BLK, dtype=jnp.int32), query_sets, query_lens))
    return (profile.reshape(NQ, L, D), similarity.reshape(NQ, N_GRP * (STEPS + 1) * TB))
```

```python
import functools
import math

import jax
import jax.numpy as jnp
from jax import lax
from jax.experimental import pallas as pl
from jax.experimental.pallas import tpu as pltpu
from jax.sharding import PartitionSpec as P

STEPS = 3
MESH = pl.DeviceIdType.MESH
LOW = -1e30


def from_behind(array, axis, by):
    length = lax.axis_size(axis)
    return lax.ppermute(array, axis, [(i, (i + by) % length) for i in range(length)])


def align_pair(query_rows, query_len, target_rows, target_len):
    scale = 3.0 / math.sqrt(query_rows.shape[-1])
    scores = (
        jnp.einsum("qid,mjd->qmij", query_rows, target_rows, preferred_element_type=jnp.float32)
        * scale
    )
    positions = lax.broadcasted_iota(jnp.float32, (1, query_rows.shape[1]), 1)
    row_ok = positions < query_len[:, None]
    col_ok = positions < target_len[:, None]
    row_mask = row_ok[:, None, :, None]
    col_mask = col_ok[None, :, None, :]
    row_top = jnp.max(jnp.where(col_mask, scores, -jnp.inf), axis=3, keepdims=True)
    row_exp = jnp.where(col_mask, jnp.exp(scores - row_top), 0.0)
    row_soft = jnp.where(row_mask, row_exp / jnp.sum(row_exp, axis=3, keepdims=True), 0.0)
    col_top = jnp.max(jnp.where(row_mask, scores, -jnp.inf), axis=2, keepdims=True)
    col_exp = jnp.where(row_mask, jnp.exp(scores - col_top), 0.0)
    col_soft = jnp.where(col_mask, col_exp / jnp.sum(col_exp, axis=2, keepdims=True), 0.0)
    weights = row_soft + col_soft - row_soft * col_soft
    similarity = jnp.sum(weights * scores, axis=(2, 3)) / jnp.sum(weights, axis=(2, 3))
    profile = jnp.einsum(
        "qmij,mjd->qid",
        row_soft.astype(jnp.bfloat16),
        target_rows,
        preferred_element_type=jnp.float32,
    )
    return (similarity, profile)


def ring_shards(queries, query_lengths, targets, target_lengths):
    blocks = targets.shape[0]
    group_size = lax.axis_size("grp")
    profile_scale = 1.0 / math.sqrt(group_size * blocks * (STEPS + 1))
    resident = (targets, target_lengths.astype(jnp.bfloat16))
    running = jnp.zeros(queries.shape, jnp.float32)
    arrived = [resident] + [
        from_behind((resident[0], resident[1]), "blk", offset) for offset in range(1, STEPS + 1)
    ]
    query_len = query_lengths.astype(jnp.float32)
    collected = []
    for visiting in arrived:
        pair_sim, pair_prof = align_pair(
            queries, query_len, visiting[0], visiting[1].astype(jnp.float32)
        )
        running = running + pair_prof
        collected.append(pair_sim)
    similarity = jnp.concatenate(collected, axis=1)
    shares = lax.psum_scatter(running, "grp", scatter_dimension=1, tiled=True) * profile_scale
    return (shares, similarity)


def remote(src, dst, sems, k, device):
    return pltpu.make_async_remote_copy(
        src_ref=src,
        dst_ref=dst,
        send_sem=sems.at[0, k],
        recv_sem=sems.at[1, k],
        device_id=device,
        device_id_type=MESH,
    )


def kernel(
    scale, profile_scale,
    ql_ref, tl_ref, q_hbm, t_hbm, prof_ref, sim_ref,
    q_buf, t_buf, ql_buf, tl_buf, a_buf, r_buf, rx_a, rx_b, rx_c, rx_z, tx_s, rx_s,
    local_sems, q_sems, l_sems, r_sems, z_sems, s_sems,
):
    res, wide = q_buf.shape[1:]
    per_core = t_buf.shape[1]
    blk, grp = lax.axis_index("blk"), lax.axis_index("grp")
    x, y = blk % 2, blk // 2
    c, z = grp % 2, grp // 2
    other_x, other_y = y * 2 + (1 - x), (1 - y) * 2 + x
    near = other_x * (1 - c) + other_y * c
    far = other_y * (1 - c) + other_x * c
    blks = (blk, near, far, 3 - blk)
    sibling = z * 2 + (1 - c)

    barrier = pltpu.get_barrier_semaphore()
    partners = [(b, grp) for b in blks[1:]] + [(b, sibling) for b in blks]
    for step in range(1, 4):
        there = (z + step) % 4
        partners += [(blk, there * 2 + c), (blk, there * 2 + (1 - c))]
    for partner in partners:
        pl.semaphore_signal(barrier, inc=1, device_id=partner, device_id_type=MESH)

    load_q = pltpu.make_async_copy(q_hbm.at[c], q_buf.at[0], local_sems.at[0])
    load_t = pltpu.make_async_copy(t_hbm, t_buf.at[0], local_sems.at[1])
    load_q.start()
    load_t.start()
    ql_buf[0] = jnp.full((8, 128), ql_ref[c], jnp.int32)
    line = lax.broadcasted_iota(jnp.int32, (8, 128), 0)
    lengths = jnp.zeros((8, 128), jnp.int32)
    for r in range(per_core):
        lengths = jnp.where(line == r, tl_ref[r], lengths)
    tl_buf[0] = lengths
    pl.semaphore_wait(barrier, len(partners))

    send_near = remote(q_hbm.at[c], q_buf.at[1], q_sems, 0, (near, grp))
    send_far = remote(q_hbm.at[c], q_buf.at[2], q_sems, 1, (far, grp))
    send_t = remote(t_hbm, t_buf.at[1], q_sems, 3, (blk, sibling))
    pass_on = remote(q_buf.at[1], q_buf.at[3], q_sems, 2, (far, grp))
    send_near.start()
    send_far.start()
    send_t.start()
    send_len = [
        remote(ql_buf.at[0], ql_buf.at[s], l_sems, s - 1, (blks[s], grp)) for s in range(1, 4)
    ]
    send_len.append(remote(tl_buf.at[0], tl_buf.at[1], l_sems, 3, (blk, sibling)))
    for copy in send_len:
        copy.start()

    lane = lax.broadcasted_iota(jnp.int32, (8, 128), 1)
    col_at = lax.broadcasted_iota(jnp.int32, (res, res), 1)
    row_at = lax.broadcasted_iota(jnp.int32, (res, res), 0)

    def align(s, h):
        scores_all = lax.dot_general(
            q_buf[s],
            t_buf[h].reshape(per_core * res, wide),
            (((1,), (1,)), ((), ())),
            preferred_element_type=jnp.float32,
        ) * scale
        row_ok = row_at < ql_buf[s, 0:1, :]
        row_ok_vec = row_ok[:, 0:1]
        place = ((blks[s] - blk + 4) % 4) * per_core
        tile = jnp.zeros((8, 128), jnp.float32)
        for r in range(per_core):
            scores = scores_all[:, r * res : (r + 1) * res]
            col_ok = col_at < tl_buf[h, r : r + 1, :]
            by_row = jnp.where(col_ok, scores, LOW)
            row_exp = jnp.exp(by_row - jnp.max(by_row, axis=1, keepdims=True))
            row_inv = jnp.where(row_ok_vec, 1.0 / jnp.sum(row_exp, axis=1, keepdims=True), 0.0)
            row_soft = row_exp * row_inv
            by_col = jnp.where(row_ok, scores, LOW)
            col_exp = jnp.exp(by_col - jnp.max(by_col, axis=0, keepdims=True))
            col_inv = jnp.where(
                col_ok[0:1, :], 1.0 / jnp.sum(col_exp, axis=0, keepdims=True), 0.0
            )
            col_soft = col_exp * col_inv
            weights = row_soft + col_soft - row_soft * col_soft
            upper = jnp.sum(
                jnp.sum(weights * scores, axis=0, keepdims=True), axis=1, keepdims=True
            )
            lower = jnp.sum(jnp.sum(weights, axis=0, keepdims=True), axis=1, keepdims=True)
            tile = jnp.where((line == c) & (lane == place + r), upper / lower, tile)
            a_buf[h, :, r * res : (r + 1) * res] = row_soft.astype(jnp.bfloat16)
        tx_s[s, h] = tile

    def profile(s):
        step = 256

        def body(n, carry):
            cols = pl.ds(pl.multiple_of(n * step, step), step)
            r_buf[s, :, cols] = sum(
                jnp.dot(
                    a_buf[h],
                    t_buf[h, :, :, cols].reshape(per_core * res, step),
                    preferred_element_type=jnp.float32,
                )
                for h in range(2)
            )
            return carry

        lax.fori_loop(0, wide // step, body, 0)

    def both(s):
        def body(h, carry):
            align(s, h)
            return carry

        lax.fori_loop(0, 2, body, 0)
        profile(s)

    def send_sim(s):
        out = []
        for h in range(2):
            if s or h:
                copy = remote(
                    tx_s.at[s, h], rx_s.at[s, h], s_sems, s * 2 + h,
                    (blks[s], sibling if h else grp),
                )
                copy.start()
                out.append(copy)
        return out

    load_q.wait()
    load_t.wait()
    send_t.wait_recv()
    send_len[3].wait_recv()
    both(0)
    sims = send_sim(0)

    send_near.wait_recv()
    pass_on.start()
    send_len[0].wait_recv()
    both(1)
    send_a = remote(r_buf.at[1], rx_a, r_sems, 0, (near, grp))
    send_a.start()
    sims += send_sim(1)

    send_far.wait_recv()
    send_len[1].wait_recv()
    both(2)
    sims += send_sim(2)

    pass_on.wait_recv()
    send_len[2].wait_recv()
    both(3)

    quarter = res // 4
    half = quarter // 2

    def chunk(i):
        return (z + 1 + i) % 4

    def rows(i):
        return pl.ds(pl.multiple_of(chunk(i) * quarter, quarter), quarter)

    send_b, send_c, send_z = [], [], []
    for i in range(4):
        send_b.append(
            remote(r_buf.at[3, rows(i)], rx_b.at[rows(i)], r_sems, 1 + i, (near, grp))
        )
        send_b[i].start()
    sims += send_sim(3)

    def finish(i):
        if i == 0:
            send_a.wait_recv()
        send_c[i].wait_recv()
        r_buf[0, rows(i), :] = r_buf[0, rows(i), :] + rx_a[rows(i), :] + rx_c[rows(i), :]
        for u in range(2):
            core = 1 - c if u else c
            there = chunk(i) * 2 + core
            if i < 3 or u:
                mine = pl.ds(pl.multiple_of(there * half, half), half)
                copy = remote(
                    r_buf.at[0, mine], rx_z.at[i, u], z_sems, i * 2 + u, (blk, there)
                )
                copy.start()
                send_z.append(copy)

    for i in range(4):
        send_b[i].wait_recv()
        r_buf[2, rows(i), :] = r_buf[2, rows(i), :] + rx_b[rows(i), :]
        send_c.append(
            remote(r_buf.at[2, rows(i)], rx_c.at[rows(i)], r_sems, 5 + i, (far, grp))
        )
        send_c[i].start()
        if i:
            finish(i - 1)
    finish(3)

    total = tx_s[0, 0]
    for copy in sims:
        copy.wait_recv()
    for s in range(4):
        for h in range(2):
            if s or h:
                total = total + rx_s[s, h]
    sim_ref[...] = total[0:2, 0 : sim_ref.shape[1]]

    for copy in send_z:
        copy.wait_recv()
    own = pl.ds(pl.multiple_of(grp * half, half), half)
    prof_ref[c] = (
        r_buf[0, own, :] + rx_z[0, 0] + rx_z[1, 0] + rx_z[2, 0]
    ) * profile_scale
    prof_ref[1 - c] = (
        rx_z[0, 1] + rx_z[1, 1] + rx_z[2, 1] + rx_z[3, 1]
    ) * profile_scale

    for copy in (
        [send_near, send_far, send_t, pass_on, send_a] + send_len + sims + send_b + send_c + send_z
    ):
        copy.wait_send()


def plane_shards(queries, query_lengths, targets, target_lengths):
    sets, res, wide = queries.shape
    per_core = targets.shape[0]
    scale = 3.0 / math.sqrt(wide)
    profile_scale = 1.0 / math.sqrt(lax.axis_size("grp") * per_core * (STEPS + 1))
    part = res // lax.axis_size("grp")
    f32, bf16 = jnp.float32, jnp.bfloat16
    vmem = pltpu.VMEM
    return pl.pallas_call(
        functools.partial(kernel, scale, profile_scale),
        out_shape=(
            jax.ShapeDtypeStruct((sets, part, wide), f32),
            jax.ShapeDtypeStruct((sets, (STEPS + 1) * per_core), f32),
        ),
        in_specs=[
            pl.BlockSpec(memory_space=pltpu.SMEM),
            pl.BlockSpec(memory_space=pltpu.SMEM),
            pl.BlockSpec(memory_space=pl.ANY),
            pl.BlockSpec(memory_space=pl.ANY),
        ],
        out_specs=(pl.BlockSpec(memory_space=vmem), pl.BlockSpec(memory_space=vmem)),
        scratch_shapes=[
            vmem((4, res, wide), bf16),
            vmem((2, per_core, res, wide), bf16),
            vmem((4, 8, 128), jnp.int32),
            vmem((2, 8, 128), jnp.int32),
            vmem((2, res, per_core * res), bf16),
            vmem((4, res, wide), f32),
            vmem((res, wide), f32),
            vmem((res, wide), f32),
            vmem((res, wide), f32),
            vmem((4, 2, part, wide), f32),
            vmem((4, 2, 8, 128), f32),
            vmem((4, 2, 8, 128), f32),
            pltpu.SemaphoreType.DMA((2,)),
            pltpu.SemaphoreType.DMA((2, 4)),
            pltpu.SemaphoreType.DMA((2, 4)),
            pltpu.SemaphoreType.DMA((2, 9)),
            pltpu.SemaphoreType.DMA((2, 8)),
            pltpu.SemaphoreType.DMA((2, 8)),
        ],
        compiler_params=pltpu.CompilerParams(
            collective_id=0, has_side_effects=True, vmem_limit_bytes=40 * 1024 * 1024
        ),
    )(query_lengths, target_lengths, queries, targets)


def solution(mesh):
    in_specs = (P("blk", None, None), P("blk"), P(("blk", "grp"), None, None), P(("blk", "grp")))
    out_specs = (P("blk", "grp", None), P("blk", "grp"))
    plane = mesh.shape["blk"] == STEPS + 1 == 4 and mesh.shape["grp"] == 8
    shards = plane_shards if plane else ring_shards
    return jax.shard_map(shards, mesh=mesh, in_specs=in_specs, out_specs=out_specs, check_vma=False)
```

```python
import functools
import math

import jax
import jax.numpy as jnp
from jax import lax
from jax.experimental import pallas as pl
from jax.experimental.pallas import tpu as pltpu
from jax.sharding import PartitionSpec as P

STEPS = 3
MESH = pl.DeviceIdType.MESH
LOW = -1e30
CODES = 32000.0


def from_behind(array, axis, by):
    length = lax.axis_size(axis)
    return lax.ppermute(array, axis, [(i, (i + by) % length) for i in range(length)])


def align_pair(query_rows, query_len, target_rows, target_len):
    scale = 3.0 / math.sqrt(query_rows.shape[-1])
    scores = (
        jnp.einsum("qid,mjd->qmij", query_rows, target_rows, preferred_element_type=jnp.float32)
        * scale
    )
    positions = lax.broadcasted_iota(jnp.float32, (1, query_rows.shape[1]), 1)
    row_ok = positions < query_len[:, None]
    col_ok = positions < target_len[:, None]
    row_mask = row_ok[:, None, :, None]
    col_mask = col_ok[None, :, None, :]
    row_top = jnp.max(jnp.where(col_mask, scores, -jnp.inf), axis=3, keepdims=True)
    row_exp = jnp.where(col_mask, jnp.exp(scores - row_top), 0.0)
    row_soft = jnp.where(row_mask, row_exp / jnp.sum(row_exp, axis=3, keepdims=True), 0.0)
    col_top = jnp.max(jnp.where(row_mask, scores, -jnp.inf), axis=2, keepdims=True)
    col_exp = jnp.where(row_mask, jnp.exp(scores - col_top), 0.0)
    col_soft = jnp.where(col_mask, col_exp / jnp.sum(col_exp, axis=2, keepdims=True), 0.0)
    weights = row_soft + col_soft - row_soft * col_soft
    similarity = jnp.sum(weights * scores, axis=(2, 3)) / jnp.sum(weights, axis=(2, 3))
    profile = jnp.einsum(
        "qmij,mjd->qid",
        row_soft.astype(jnp.bfloat16),
        target_rows,
        preferred_element_type=jnp.float32,
    )
    return (similarity, profile)


def ring_shards(queries, query_lengths, targets, target_lengths):
    blocks = targets.shape[0]
    group_size = lax.axis_size("grp")
    profile_scale = 1.0 / math.sqrt(group_size * blocks * (STEPS + 1))
    resident = (targets, target_lengths.astype(jnp.bfloat16))
    running = jnp.zeros(queries.shape, jnp.float32)
    arrived = [resident] + [
        from_behind((resident[0], resident[1]), "blk", offset) for offset in range(1, STEPS + 1)
    ]
    query_len = query_lengths.astype(jnp.float32)
    collected = []
    for visiting in arrived:
        pair_sim, pair_prof = align_pair(
            queries, query_len, visiting[0], visiting[1].astype(jnp.float32)
        )
        running = running + pair_prof
        collected.append(pair_sim)
    similarity = jnp.concatenate(collected, axis=1)
    shares = lax.psum_scatter(running, "grp", scatter_dimension=1, tiled=True) * profile_scale
    return (shares, similarity)


def remote(src, dst, sems, k, device):
    return pltpu.make_async_remote_copy(
        src_ref=src,
        dst_ref=dst,
        send_sem=sems.at[0, k],
        recv_sem=sems.at[1, k],
        device_id=device,
        device_id_type=MESH,
    )


def encode(dst, at, values):
    wide = values.shape[1]
    top = jnp.maximum(jnp.max(jnp.abs(values), axis=1, keepdims=True), 2.0**-110)
    power = jnp.ceil(jnp.log2(top) * 64.0)
    factor = jnp.exp2(power * (-1.0 / 64.0)) * CODES
    dst[at, 0:wide] = jnp.round(values * factor).astype(jnp.int32).astype(jnp.int16)
    dst[at, wide:] = (
        jnp.broadcast_to(power, (values.shape[0], 128)).astype(jnp.int32).astype(jnp.int16)
    )


def decode(coded):
    wide = coded.shape[1] - 128
    power = coded[:, wide:].astype(jnp.int32).astype(jnp.float32)
    factor = jnp.exp2(power * (1.0 / 64.0)) * (1.0 / CODES)
    values = coded[:, 0:wide].astype(jnp.int32).astype(jnp.float32)
    return values * jnp.concatenate([factor] * (wide // 128), axis=1)


def kernel(
    scale, profile_scale,
    ql_hbm, tl_hbm, q_hbm, t_hbm, prof_ref, sim_ref,
    q_buf, t_buf, ql_buf, tl_buf, a_buf, r_buf, tx_a, tx_b, tx_c, tx_z, rx_a, rx_b, rx_c, rx_z,
    tx_s, rx_s, ql_ref, tl_ref,
    local_sems, q_sems, l_sems, r_sems, z_sems, s_sems,
):
    res, wide = q_buf.shape[1:]
    per_core = t_buf.shape[1]
    blk, grp = lax.axis_index("blk"), lax.axis_index("grp")
    x, y = blk % 2, blk // 2
    c, z = grp % 2, grp // 2
    other_x, other_y = y * 2 + (1 - x), (1 - y) * 2 + x
    near = other_x * (1 - c) + other_y * c
    far = other_y * (1 - c) + other_x * c
    blks = (blk, near, far, 3 - blk)
    sibling = z * 2 + (1 - c)

    barrier = pltpu.get_barrier_semaphore()
    partners = [(b, grp) for b in blks[1:]] + [(b, sibling) for b in blks]
    for step in range(1, 4):
        there = (z + step) % 4
        partners += [(blk, there * 2 + c), (blk, there * 2 + (1 - c))]
    for partner in partners:
        pl.semaphore_signal(barrier, inc=1, device_id=partner, device_id_type=MESH)

    load_q = pltpu.make_async_copy(q_hbm.at[c], q_buf.at[0], local_sems.at[0])
    load_t = pltpu.make_async_copy(t_hbm, t_buf.at[0], local_sems.at[1])
    load_ql = pltpu.make_async_copy(ql_hbm, ql_ref, local_sems.at[2])
    load_tl = pltpu.make_async_copy(tl_hbm, tl_ref, local_sems.at[3])
    load_ql.start()
    load_tl.start()
    load_q.start()
    load_t.start()
    load_ql.wait()
    load_tl.wait()
    ql_buf[0] = jnp.full((8, 128), ql_ref[c], jnp.int32)
    line = lax.broadcasted_iota(jnp.int32, (8, 128), 0)
    lengths = jnp.zeros((8, 128), jnp.int32)
    for r in range(per_core):
        lengths = jnp.where(line == r, tl_ref[r], lengths)
    tl_buf[0] = lengths
    pl.semaphore_wait(barrier, len(partners))

    send_near = remote(q_hbm.at[c], q_buf.at[1], q_sems, 0, (near, grp))
    send_far = remote(q_hbm.at[c], q_buf.at[2], q_sems, 1, (far, grp))
    send_t = remote(t_hbm, t_buf.at[1], q_sems, 3, (blk, sibling))
    pass_on = remote(q_buf.at[1], q_buf.at[3], q_sems, 2, (far, grp))
    send_near.start()
    send_far.start()
    send_t.start()
    send_len = [
        remote(ql_buf.at[0], ql_buf.at[s], l_sems, s - 1, (blks[s], grp)) for s in range(1, 4)
    ]
    send_len.append(remote(tl_buf.at[0], tl_buf.at[1], l_sems, 3, (blk, sibling)))
    for copy in send_len:
        copy.start()

    lane = lax.broadcasted_iota(jnp.int32, (8, 128), 1)
    col_at = lax.broadcasted_iota(jnp.int32, (res, res), 1)
    row_at = lax.broadcasted_iota(jnp.int32, (res, res), 0)

    def align(s, h):
        scores_all = lax.dot_general(
            q_buf[s],
            t_buf[h].reshape(per_core * res, wide),
            (((1,), (1,)), ((), ())),
            preferred_element_type=jnp.float32,
        ) * scale
        row_ok = row_at < ql_buf[s, 0:1, :]
        row_ok_vec = row_ok[:, 0:1]
        place = ((blks[s] - blk + 4) % 4) * per_core
        tile = jnp.zeros((8, 128), jnp.float32)
        for r in range(per_core):
            scores = scores_all[:, r * res : (r + 1) * res]
            col_ok = col_at < tl_buf[h, r : r + 1, :]
            by_row = jnp.where(col_ok, scores, LOW)
            row_exp = jnp.exp(by_row - jnp.max(by_row, axis=1, keepdims=True))
            row_inv = jnp.where(row_ok_vec, 1.0 / jnp.sum(row_exp, axis=1, keepdims=True), 0.0)
            row_soft = row_exp * row_inv
            by_col = jnp.where(row_ok, scores, LOW)
            col_exp = jnp.exp(by_col - jnp.max(by_col, axis=0, keepdims=True))
            col_inv = jnp.where(
                col_ok[0:1, :], 1.0 / jnp.sum(col_exp, axis=0, keepdims=True), 0.0
            )
            col_soft = col_exp * col_inv
            weights = row_soft + col_soft - row_soft * col_soft
            upper = jnp.sum(
                jnp.sum(weights * scores, axis=0, keepdims=True), axis=1, keepdims=True
            )
            lower = jnp.sum(jnp.sum(weights, axis=0, keepdims=True), axis=1, keepdims=True)
            tile = jnp.where((line == c) & (lane == place + r), upper / lower, tile)
            a_buf[h, :, r * res : (r + 1) * res] = row_soft.astype(jnp.bfloat16)
        tx_s[s, h] = tile

    def profile(s):
        step = 256

        def body(n, carry):
            cols = pl.ds(pl.multiple_of(n * step, step), step)
            r_buf[s, :, cols] = sum(
                jnp.dot(
                    a_buf[h],
                    t_buf[h, :, :, cols].reshape(per_core * res, step),
                    preferred_element_type=jnp.float32,
                )
                for h in range(2)
            )
            return carry

        lax.fori_loop(0, wide // step, body, 0)

    def both(s):
        def body(h, carry):
            align(s, h)
            return carry

        lax.fori_loop(0, 2, body, 0)
        profile(s)

    def send_sim(s):
        out = []
        for h in range(2):
            if s or h:
                copy = remote(
                    tx_s.at[s, h], rx_s.at[s, h], s_sems, s * 2 + h,
                    (blks[s], sibling if h else grp),
                )
                copy.start()
                out.append(copy)
        return out

    load_q.wait()
    load_t.wait()
    send_t.wait_recv()
    send_len[3].wait_recv()
    both(0)
    sims = send_sim(0)

    send_near.wait_recv()
    pass_on.start()
    send_len[0].wait_recv()
    both(1)
    encode(tx_a, slice(None), r_buf[1])
    send_a = remote(tx_a, rx_a, r_sems, 0, (near, grp))
    send_a.start()
    sims += send_sim(1)

    send_far.wait_recv()
    send_len[1].wait_recv()
    both(2)
    sims += send_sim(2)

    pass_on.wait_recv()
    send_len[2].wait_recv()
    both(3)

    quarter = res // 4
    half = quarter // 2

    def chunk(i):
        return (z + 1 + i) % 4

    def rows(i):
        return pl.ds(pl.multiple_of(chunk(i) * quarter, quarter), quarter)

    send_b, send_c, send_z = [], [], []
    for i in range(4):
        encode(tx_b, rows(i), r_buf[3, rows(i), :])
        send_b.append(
            remote(tx_b.at[rows(i)], rx_b.at[rows(i)], r_sems, 1 + i, (near, grp))
        )
        send_b[i].start()
    sims += send_sim(3)

    def finish(i):
        if i == 0:
            send_a.wait_recv()
        send_c[i].wait_recv()
        summed = r_buf[0, rows(i), :] + decode(rx_a[rows(i), :]) + decode(rx_c[rows(i), :])
        encode(tx_z, rows(i), summed)
        if i == 3:
            r_buf[0, rows(i), :] = summed
        for u in range(2):
            core = 1 - c if u else c
            there = chunk(i) * 2 + core
            if i < 3 or u:
                mine = pl.ds(pl.multiple_of(there * half, half), half)
                copy = remote(
                    tx_z.at[mine], rx_z.at[i, u], z_sems, i * 2 + u, (blk, there)
                )
                copy.start()
                send_z.append(copy)

    for i in range(4):
        send_b[i].wait_recv()
        encode(tx_c, rows(i), r_buf[2, rows(i), :] + decode(rx_b[rows(i), :]))
        send_c.append(
            remote(tx_c.at[rows(i)], rx_c.at[rows(i)], r_sems, 5 + i, (far, grp))
        )
        send_c[i].start()
        if i:
            finish(i - 1)
    finish(3)

    total = tx_s[0, 0]
    for copy in sims:
        copy.wait_recv()
    for s in range(4):
        for h in range(2):
            if s or h:
                total = total + rx_s[s, h]
    sim_ref[...] = total[0:2, 0 : sim_ref.shape[1]]

    for copy in send_z:
        copy.wait_recv()
    own = pl.ds(pl.multiple_of(grp * half, half), half)
    prof_ref[c] = (
        r_buf[0, own, :] + decode(rx_z[0, 0]) + decode(rx_z[1, 0]) + decode(rx_z[2, 0])
    ) * profile_scale
    prof_ref[1 - c] = (
        decode(rx_z[0, 1]) + decode(rx_z[1, 1]) + decode(rx_z[2, 1]) + decode(rx_z[3, 1])
    ) * profile_scale

    for copy in (
        [send_near, send_far, send_t, pass_on, send_a] + send_len + sims + send_b + send_c + send_z
    ):
        copy.wait_send()


def plane_shards(queries, query_lengths, targets, target_lengths):
    sets, res, wide = queries.shape
    per_core = targets.shape[0]
    scale = 3.0 / math.sqrt(wide)
    profile_scale = 1.0 / math.sqrt(lax.axis_size("grp") * per_core * (STEPS + 1))
    part = res // lax.axis_size("grp")
    f32, bf16 = jnp.float32, jnp.bfloat16
    vmem = pltpu.VMEM
    return pl.pallas_call(
        functools.partial(kernel, scale, profile_scale),
        out_shape=(
            jax.ShapeDtypeStruct((sets, part, wide), f32),
            jax.ShapeDtypeStruct((sets, (STEPS + 1) * per_core), f32),
        ),
        in_specs=[
            pl.BlockSpec(memory_space=pl.ANY),
            pl.BlockSpec(memory_space=pl.ANY),
            pl.BlockSpec(memory_space=pl.ANY),
            pl.BlockSpec(memory_space=pl.ANY),
        ],
        out_specs=(pl.BlockSpec(memory_space=vmem), pl.BlockSpec(memory_space=vmem)),
        scratch_shapes=[
            vmem((4, res, wide), bf16),
            vmem((2, per_core, res, wide), bf16),
            vmem((4, 8, 128), jnp.int32),
            vmem((2, 8, 128), jnp.int32),
            vmem((2, res, per_core * res), bf16),
            vmem((4, res, wide), f32),
            *[vmem((res, wide + 128), jnp.int16) for _ in range(7)],
            vmem((4, 2, part, wide + 128), jnp.int16),
            vmem((4, 2, 8, 128), f32),
            vmem((4, 2, 8, 128), f32),
            pltpu.SMEM(query_lengths.shape, jnp.int32),
            pltpu.SMEM(target_lengths.shape, jnp.int32),
            pltpu.SemaphoreType.DMA((4,)),
            pltpu.SemaphoreType.DMA((2, 4)),
            pltpu.SemaphoreType.DMA((2, 4)),
            pltpu.SemaphoreType.DMA((2, 9)),
            pltpu.SemaphoreType.DMA((2, 8)),
            pltpu.SemaphoreType.DMA((2, 8)),
        ],
        compiler_params=pltpu.CompilerParams(
            collective_id=0, has_side_effects=True, vmem_limit_bytes=60 * 1024 * 1024
        ),
    )(query_lengths, target_lengths, queries, targets)


def solution(mesh):
    in_specs = (P("blk", None, None), P("blk"), P(("blk", "grp"), None, None), P(("blk", "grp")))
    out_specs = (P("blk", "grp", None), P("blk", "grp"))
    plane = mesh.shape["blk"] == STEPS + 1 == 4 and mesh.shape["grp"] == 8
    shards = plane_shards if plane else ring_shards
    return jax.shard_map(shards, mesh=mesh, in_specs=in_specs, out_specs=out_specs, check_vma=False)
```

```python
import functools
import math

import jax
import jax.numpy as jnp
from jax import lax
from jax.experimental import pallas as pl
from jax.experimental.pallas import tpu as pltpu
from jax.sharding import PartitionSpec as P

STEPS = 3
MESH = pl.DeviceIdType.MESH
LOW = -1e30
CODES = 32000.0


def from_behind(array, axis, by):
    length = lax.axis_size(axis)
    return lax.ppermute(array, axis, [(i, (i + by) % length) for i in range(length)])


def align_pair(query_rows, query_len, target_rows, target_len):
    scale = 3.0 / math.sqrt(query_rows.shape[-1])
    scores = (
        jnp.einsum("qid,mjd->qmij", query_rows, target_rows, preferred_element_type=jnp.float32)
        * scale
    )
    positions = lax.broadcasted_iota(jnp.float32, (1, query_rows.shape[1]), 1)
    row_ok = positions < query_len[:, None]
    col_ok = positions < target_len[:, None]
    row_mask = row_ok[:, None, :, None]
    col_mask = col_ok[None, :, None, :]
    row_top = jnp.max(jnp.where(col_mask, scores, -jnp.inf), axis=3, keepdims=True)
    row_exp = jnp.where(col_mask, jnp.exp(scores - row_top), 0.0)
    row_soft = jnp.where(row_mask, row_exp / jnp.sum(row_exp, axis=3, keepdims=True), 0.0)
    col_top = jnp.max(jnp.where(row_mask, scores, -jnp.inf), axis=2, keepdims=True)
    col_exp = jnp.where(row_mask, jnp.exp(scores - col_top), 0.0)
    col_soft = jnp.where(col_mask, col_exp / jnp.sum(col_exp, axis=2, keepdims=True), 0.0)
    weights = row_soft + col_soft - row_soft * col_soft
    similarity = jnp.sum(weights * scores, axis=(2, 3)) / jnp.sum(weights, axis=(2, 3))
    profile = jnp.einsum(
        "qmij,mjd->qid",
        row_soft.astype(jnp.bfloat16),
        target_rows,
        preferred_element_type=jnp.float32,
    )
    return (similarity, profile)


def ring_shards(queries, query_lengths, targets, target_lengths):
    blocks = targets.shape[0]
    group_size = lax.axis_size("grp")
    profile_scale = 1.0 / math.sqrt(group_size * blocks * (STEPS + 1))
    resident = (targets, target_lengths.astype(jnp.bfloat16))
    running = jnp.zeros(queries.shape, jnp.float32)
    arrived = [resident] + [
        from_behind((resident[0], resident[1]), "blk", offset) for offset in range(1, STEPS + 1)
    ]
    query_len = query_lengths.astype(jnp.float32)
    collected = []
    for visiting in arrived:
        pair_sim, pair_prof = align_pair(
            queries, query_len, visiting[0], visiting[1].astype(jnp.float32)
        )
        running = running + pair_prof
        collected.append(pair_sim)
    similarity = jnp.concatenate(collected, axis=1)
    shares = lax.psum_scatter(running, "grp", scatter_dimension=1, tiled=True) * profile_scale
    return (shares, similarity)


def remote(src, dst, sems, k, device):
    return pltpu.make_async_remote_copy(
        src_ref=src,
        dst_ref=dst,
        send_sem=sems.at[0, k],
        recv_sem=sems.at[1, k],
        device_id=device,
        device_id_type=MESH,
    )


def encode(dst, at, values):
    wide = values.shape[1]
    top = jnp.maximum(jnp.max(jnp.abs(values), axis=1, keepdims=True), 2.0**-110)
    power = jnp.ceil(jnp.log2(top) * 64.0)
    factor = jnp.exp2(power * (-1.0 / 64.0)) * CODES
    dst[at, 0:wide] = jnp.round(values * factor).astype(jnp.int32).astype(jnp.int16)
    dst[at, wide:] = (
        jnp.broadcast_to(power, (values.shape[0], 128)).astype(jnp.int32).astype(jnp.int16)
    )


def decode(coded):
    wide = coded.shape[1] - 128
    power = coded[:, wide:].astype(jnp.int32).astype(jnp.float32)
    factor = jnp.exp2(power * (1.0 / 64.0)) * (1.0 / CODES)
    values = coded[:, 0:wide].astype(jnp.int32).astype(jnp.float32)
    return values * jnp.concatenate([factor] * (wide // 128), axis=1)


def kernel(
    scale, profile_scale,
    ql_hbm, tl_hbm, q_hbm, t_hbm, prof_ref, sim_ref,
    q_buf, t_buf, ql_buf, tl_buf, s_buf, w_buf, a_buf, r_buf, tx_a, tx_b, tx_c, tx_z, rx_a, rx_b, rx_c, rx_z,
    tx_s, rx_s, ql_ref, tl_ref,
    local_sems, q_sems, l_sems, r_sems, z_sems, s_sems,
):
    res, wide = q_buf.shape[1:]
    per_core = t_buf.shape[1]
    blk, grp = lax.axis_index("blk"), lax.axis_index("grp")
    x, y = blk % 2, blk // 2
    c, z = grp % 2, grp // 2
    other_x, other_y = y * 2 + (1 - x), (1 - y) * 2 + x
    near = other_x * (1 - c) + other_y * c
    far = other_y * (1 - c) + other_x * c
    blks = (blk, near, far, 3 - blk)
    sibling = z * 2 + (1 - c)

    barrier = pltpu.get_barrier_semaphore()
    partners = [(b, grp) for b in blks[1:]] + [(b, sibling) for b in blks]
    for step in range(1, 4):
        there = (z + step) % 4
        partners += [(blk, there * 2 + c), (blk, there * 2 + (1 - c))]
    for partner in partners:
        pl.semaphore_signal(barrier, inc=1, device_id=partner, device_id_type=MESH)

    load_q = pltpu.make_async_copy(q_hbm.at[c], q_buf.at[0], local_sems.at[0])
    load_t = pltpu.make_async_copy(t_hbm, t_buf.at[0], local_sems.at[1])
    load_ql = pltpu.make_async_copy(ql_hbm, ql_ref, local_sems.at[2])
    load_tl = pltpu.make_async_copy(tl_hbm, tl_ref, local_sems.at[3])
    load_ql.start()
    load_tl.start()
    load_q.start()
    load_t.start()
    load_ql.wait()
    load_tl.wait()
    ql_buf[0] = jnp.full((8, 128), ql_ref[c], jnp.int32)
    line = lax.broadcasted_iota(jnp.int32, (8, 128), 0)
    lengths = jnp.zeros((8, 128), jnp.int32)
    for r in range(per_core):
        lengths = jnp.where(line == r, tl_ref[r], lengths)
    tl_buf[0] = lengths
    pl.semaphore_wait(barrier, len(partners))

    split = res // 2
    halves = [pl.ds(0, split), pl.ds(split, split)]
    send_near = [
        remote(q_hbm.at[c, part], q_buf.at[1, part], q_sems, n, (near, grp))
        for n, part in enumerate(halves)
    ]
    pass_on = [
        remote(q_buf.at[1, part], q_buf.at[3, part], q_sems, 2 + n, (far, grp))
        for n, part in enumerate(halves)
    ]
    send_far = remote(q_hbm.at[c], q_buf.at[2], q_sems, 4, (far, grp))
    send_t = remote(t_hbm, t_buf.at[1], q_sems, 5, (blk, sibling))
    for copy in send_near:
        copy.start()
    send_t.start()
    send_len = [
        remote(ql_buf.at[0], ql_buf.at[s], l_sems, s - 1, (blks[s], grp)) for s in range(1, 4)
    ]
    send_len.append(remote(tl_buf.at[0], tl_buf.at[1], l_sems, 3, (blk, sibling)))
    for copy in send_len:
        copy.start()

    lane = lax.broadcasted_iota(jnp.int32, (8, 128), 1)
    col_at = lax.broadcasted_iota(jnp.int32, (res, res), 1)
    row_at = lax.broadcasted_iota(jnp.int32, (res, res), 0)

    def align(s, h):
        scores_all = lax.dot_general(
            q_buf[s],
            t_buf[h].reshape(per_core * res, wide),
            (((1,), (1,)), ((), ())),
            preferred_element_type=jnp.float32,
        ) * scale
        row_ok_vec = (row_at < ql_buf[s, 0:1, :])[:, 0:1]
        for r in range(per_core):
            cols = slice(r * res, (r + 1) * res)
            scores = scores_all[:, cols]
            s_buf[s, h, :, cols] = scores
            by_row = jnp.where(col_at < tl_buf[h, r : r + 1, :], scores, LOW)
            row_exp = jnp.exp(by_row - jnp.max(by_row, axis=1, keepdims=True))
            row_inv = jnp.where(row_ok_vec, 1.0 / jnp.sum(row_exp, axis=1, keepdims=True), 0.0)
            row_soft = row_exp * row_inv
            w_buf[s, h, :, cols] = row_soft
            a_buf[h, :, cols] = row_soft.astype(jnp.bfloat16)

    def similar(s, h):
        row_ok = row_at < ql_buf[s, 0:1, :]
        place = ((blks[s] - blk + 4) % 4) * per_core
        tile = jnp.zeros((8, 128), jnp.float32)
        for r in range(per_core):
            cols = slice(r * res, (r + 1) * res)
            scores = s_buf[s, h, :, cols]
            row_soft = w_buf[s, h, :, cols]
            by_col = jnp.where(row_ok, scores, LOW)
            col_exp = jnp.exp(by_col - jnp.max(by_col, axis=0, keepdims=True))
            col_inv = jnp.where(
                col_at[0:1, :] < tl_buf[h, r : r + 1, :],
                1.0 / jnp.sum(col_exp, axis=0, keepdims=True),
                0.0,
            )
            col_soft = col_exp * col_inv
            weights = row_soft + col_soft - row_soft * col_soft
            upper = jnp.sum(
                jnp.sum(weights * scores, axis=0, keepdims=True), axis=1, keepdims=True
            )
            lower = jnp.sum(jnp.sum(weights, axis=0, keepdims=True), axis=1, keepdims=True)
            tile = jnp.where((line == c) & (lane == place + r), upper / lower, tile)
        tx_s[s, h] = tile

    def profile(s):
        step = 256

        def body(n, carry):
            cols = pl.ds(pl.multiple_of(n * step, step), step)
            r_buf[s, :, cols] = sum(
                jnp.dot(
                    a_buf[h],
                    t_buf[h, :, :, cols].reshape(per_core * res, step),
                    preferred_element_type=jnp.float32,
                )
                for h in range(2)
            )
            return carry

        lax.fori_loop(0, wide // step, body, 0)

    def both(s):
        def body(h, carry):
            align(s, h)
            return carry

        lax.fori_loop(0, 2, body, 0)
        profile(s)

    def similarities(s):
        def body(h, carry):
            similar(s, h)
            return carry

        lax.fori_loop(0, 2, body, 0)
        out = []
        for h in range(2):
            if s or h:
                copy = remote(
                    tx_s.at[s, h], rx_s.at[s, h], s_sems, s * 2 + h,
                    (blks[s], sibling if h else grp),
                )
                copy.start()
                out.append(copy)
        return out

    load_q.wait()
    load_t.wait()
    align(0, 0)
    for n in range(2):
        send_near[n].wait_recv()
        pass_on[n].start()
    send_far.start()
    send_t.wait_recv()
    send_len[3].wait_recv()
    align(0, 1)
    profile(0)

    send_len[0].wait_recv()
    both(1)
    encode(tx_a, slice(None), r_buf[1])
    send_a = remote(tx_a, rx_a, r_sems, 0, (near, grp))
    send_a.start()

    for n in range(2):
        pass_on[n].wait_recv()
    send_len[2].wait_recv()
    both(3)

    quarter = res // 4
    half = quarter // 2

    def chunk(i):
        return (z + 1 + i) % 4

    def rows(i):
        return pl.ds(pl.multiple_of(chunk(i) * quarter, quarter), quarter)

    send_b, send_c, send_z = [], [], []
    for i in range(4):
        encode(tx_b, rows(i), r_buf[3, rows(i), :])
        send_b.append(
            remote(tx_b.at[rows(i)], rx_b.at[rows(i)], r_sems, 1 + i, (near, grp))
        )
        send_b[i].start()

    send_far.wait_recv()
    send_len[1].wait_recv()
    both(2)

    def finish(i):
        if i == 0:
            send_a.wait_recv()
        send_c[i].wait_recv()
        summed = r_buf[0, rows(i), :] + decode(rx_a[rows(i), :]) + decode(rx_c[rows(i), :])
        encode(tx_z, rows(i), summed)
        if i == 3:
            r_buf[0, rows(i), :] = summed
        for u in range(2):
            core = 1 - c if u else c
            there = chunk(i) * 2 + core
            if i < 3 or u:
                mine = pl.ds(pl.multiple_of(there * half, half), half)
                copy = remote(
                    tx_z.at[mine], rx_z.at[i, u], z_sems, i * 2 + u, (blk, there)
                )
                copy.start()
                send_z.append(copy)

    for i in range(4):
        send_b[i].wait_recv()
        encode(tx_c, rows(i), r_buf[2, rows(i), :] + decode(rx_b[rows(i), :]))
        send_c.append(
            remote(tx_c.at[rows(i)], rx_c.at[rows(i)], r_sems, 5 + i, (far, grp))
        )
        send_c[i].start()
    sims = similarities(0)
    sims += similarities(1)
    for i in range(4):
        finish(i)
    sims += similarities(2)
    sims += similarities(3)

    total = tx_s[0, 0]
    for copy in sims:
        copy.wait_recv()
    for s in range(4):
        for h in range(2):
            if s or h:
                total = total + rx_s[s, h]
    sim_ref[...] = total[0:2, 0 : sim_ref.shape[1]]

    for copy in send_z:
        copy.wait_recv()
    own = pl.ds(pl.multiple_of(grp * half, half), half)
    prof_ref[c] = (
        r_buf[0, own, :] + decode(rx_z[0, 0]) + decode(rx_z[1, 0]) + decode(rx_z[2, 0])
    ) * profile_scale
    prof_ref[1 - c] = (
        decode(rx_z[0, 1]) + decode(rx_z[1, 1]) + decode(rx_z[2, 1]) + decode(rx_z[3, 1])
    ) * profile_scale

    for copy in (
        send_near + pass_on + [send_far, send_t, send_a]
        + send_len + sims + send_b + send_c + send_z
    ):
        copy.wait_send()


def plane_shards(queries, query_lengths, targets, target_lengths):
    sets, res, wide = queries.shape
    per_core = targets.shape[0]
    scale = 3.0 / math.sqrt(wide)
    profile_scale = 1.0 / math.sqrt(lax.axis_size("grp") * per_core * (STEPS + 1))
    part = res // lax.axis_size("grp")
    f32, bf16 = jnp.float32, jnp.bfloat16
    vmem = pltpu.VMEM
    return pl.pallas_call(
        functools.partial(kernel, scale, profile_scale),
        out_shape=(
            jax.ShapeDtypeStruct((sets, part, wide), f32),
            jax.ShapeDtypeStruct((sets, (STEPS + 1) * per_core), f32),
        ),
        in_specs=[
            pl.BlockSpec(memory_space=pltpu.HBM),
            pl.BlockSpec(memory_space=pltpu.HBM),
            pl.BlockSpec(memory_space=pltpu.HBM),
            pl.BlockSpec(memory_space=pltpu.HBM),
        ],
        out_specs=(pl.BlockSpec(memory_space=vmem), pl.BlockSpec(memory_space=vmem)),
        scratch_shapes=[
            vmem((4, res, wide), bf16),
            vmem((2, per_core, res, wide), bf16),
            vmem((4, 8, 128), jnp.int32),
            vmem((2, 8, 128), jnp.int32),
            vmem((4, 2, res, per_core * res), f32),
            vmem((4, 2, res, per_core * res), f32),
            vmem((2, res, per_core * res), bf16),
            vmem((4, res, wide), f32),
            *[vmem((res, wide + 128), jnp.int16) for _ in range(7)],
            vmem((4, 2, part, wide + 128), jnp.int16),
            vmem((4, 2, 8, 128), f32),
            vmem((4, 2, 8, 128), f32),
            pltpu.SMEM(query_lengths.shape, jnp.int32),
            pltpu.SMEM(target_lengths.shape, jnp.int32),
            pltpu.SemaphoreType.DMA((4,)),
            pltpu.SemaphoreType.DMA((2, 6)),
            pltpu.SemaphoreType.DMA((2, 4)),
            pltpu.SemaphoreType.DMA((2, 9)),
            pltpu.SemaphoreType.DMA((2, 8)),
            pltpu.SemaphoreType.DMA((2, 8)),
        ],
        compiler_params=pltpu.CompilerParams(
            collective_id=0, has_side_effects=True, vmem_limit_bytes=56 * 1024 * 1024
        ),
    )(query_lengths, target_lengths, queries, targets)


def solution(mesh):
    in_specs = (P("blk", None, None), P("blk"), P(("blk", "grp"), None, None), P(("blk", "grp")))
    out_specs = (P("blk", "grp", None), P("blk", "grp"))
    plane = mesh.shape["blk"] == STEPS + 1 == 4 and mesh.shape["grp"] == 8
    shards = plane_shards if plane else ring_shards
    return jax.shard_map(shards, mesh=mesh, in_specs=in_specs, out_specs=out_specs, check_vma=False)
```

```python
import functools
import math

import jax
import jax.numpy as jnp
from jax import lax
from jax.experimental import pallas as pl
from jax.experimental.pallas import tpu as pltpu
from jax.sharding import PartitionSpec as P

STEPS = 3
MESH = pl.DeviceIdType.MESH
LOW = -1e30
CODES = 32000.0


def from_behind(array, axis, by):
    length = lax.axis_size(axis)
    return lax.ppermute(array, axis, [(i, (i + by) % length) for i in range(length)])


def align_pair(query_rows, query_len, target_rows, target_len):
    scale = 3.0 / math.sqrt(query_rows.shape[-1])
    scores = (
        jnp.einsum("qid,mjd->qmij", query_rows, target_rows, preferred_element_type=jnp.float32)
        * scale
    )
    positions = lax.broadcasted_iota(jnp.float32, (1, query_rows.shape[1]), 1)
    row_ok = positions < query_len[:, None]
    col_ok = positions < target_len[:, None]
    row_mask = row_ok[:, None, :, None]
    col_mask = col_ok[None, :, None, :]
    row_top = jnp.max(jnp.where(col_mask, scores, -jnp.inf), axis=3, keepdims=True)
    row_exp = jnp.where(col_mask, jnp.exp(scores - row_top), 0.0)
    row_soft = jnp.where(row_mask, row_exp / jnp.sum(row_exp, axis=3, keepdims=True), 0.0)
    col_top = jnp.max(jnp.where(row_mask, scores, -jnp.inf), axis=2, keepdims=True)
    col_exp = jnp.where(row_mask, jnp.exp(scores - col_top), 0.0)
    col_soft = jnp.where(col_mask, col_exp / jnp.sum(col_exp, axis=2, keepdims=True), 0.0)
    weights = row_soft + col_soft - row_soft * col_soft
    similarity = jnp.sum(weights * scores, axis=(2, 3)) / jnp.sum(weights, axis=(2, 3))
    profile = jnp.einsum(
        "qmij,mjd->qid",
        row_soft.astype(jnp.bfloat16),
        target_rows,
        preferred_element_type=jnp.float32,
    )
    return (similarity, profile)


def ring_shards(queries, query_lengths, targets, target_lengths):
    blocks = targets.shape[0]
    group_size = lax.axis_size("grp")
    profile_scale = 1.0 / math.sqrt(group_size * blocks * (STEPS + 1))
    resident = (targets, target_lengths.astype(jnp.bfloat16))
    running = jnp.zeros(queries.shape, jnp.float32)
    arrived = [resident] + [
        from_behind((resident[0], resident[1]), "blk", offset) for offset in range(1, STEPS + 1)
    ]
    query_len = query_lengths.astype(jnp.float32)
    collected = []
    for visiting in arrived:
        pair_sim, pair_prof = align_pair(
            queries, query_len, visiting[0], visiting[1].astype(jnp.float32)
        )
        running = running + pair_prof
        collected.append(pair_sim)
    similarity = jnp.concatenate(collected, axis=1)
    shares = lax.psum_scatter(running, "grp", scatter_dimension=1, tiled=True) * profile_scale
    return (shares, similarity)


def remote(src, dst, sems, k, device):
    return pltpu.make_async_remote_copy(
        src_ref=src,
        dst_ref=dst,
        send_sem=sems.at[0, k],
        recv_sem=sems.at[1, k],
        device_id=device,
        device_id_type=MESH,
    )


def encode(dst, at, values):
    wide = values.shape[1]
    top = jnp.maximum(jnp.max(jnp.abs(values), axis=1, keepdims=True), 2.0**-110)
    power = jnp.ceil(jnp.log2(top) * 64.0)
    factor = jnp.exp2(power * (-1.0 / 64.0)) * CODES
    dst[at, 0:wide] = jnp.round(values * factor).astype(jnp.int32).astype(jnp.int16)
    dst[at, wide:] = (
        jnp.broadcast_to(power, (values.shape[0], 128)).astype(jnp.int32).astype(jnp.int16)
    )


def decode(coded):
    wide = coded.shape[1] - 128
    power = coded[:, wide:].astype(jnp.int32).astype(jnp.float32)
    factor = jnp.exp2(power * (1.0 / 64.0)) * (1.0 / CODES)
    values = coded[:, 0:wide].astype(jnp.int32).astype(jnp.float32)
    return values * jnp.concatenate([factor] * (wide // 128), axis=1)


def kernel(
    scale, profile_scale,
    ql_hbm, tl_hbm, q_hbm, t_hbm, prof_ref, sim_ref,
    q_buf, t_buf, ql_buf, tl_buf, s_buf, w_buf, a_buf, r_buf, tx_a, tx_b, tx_c, tx_z, rx_a, rx_b, rx_c, rx_z,
    tx_s, rx_s, ql_ref, tl_ref,
    local_sems, q_sems, l_sems, r_sems, z_sems, s_sems,
):
    res, wide = q_buf.shape[1:]
    per_core = t_buf.shape[1]
    blk, grp = lax.axis_index("blk"), lax.axis_index("grp")
    x, y = blk % 2, blk // 2
    c, z = grp % 2, grp // 2
    other_x, other_y = y * 2 + (1 - x), (1 - y) * 2 + x
    near = other_x * (1 - c) + other_y * c
    far = other_y * (1 - c) + other_x * c
    blks = (blk, near, far, 3 - blk)
    sibling = z * 2 + (1 - c)

    barrier = pltpu.get_barrier_semaphore()
    partners = [(b, grp) for b in blks[1:]] + [(b, sibling) for b in blks]
    for step in range(1, 4):
        there = (z + step) % 4
        partners += [(blk, there * 2 + c), (blk, there * 2 + (1 - c))]
    for partner in partners:
        pl.semaphore_signal(barrier, inc=1, device_id=partner, device_id_type=MESH)

    load_q = pltpu.make_async_copy(q_hbm.at[c], q_buf.at[0], local_sems.at[0])
    load_t = pltpu.make_async_copy(t_hbm, t_buf.at[0], local_sems.at[1])
    load_ql = pltpu.make_async_copy(ql_hbm, ql_ref, local_sems.at[2])
    load_tl = pltpu.make_async_copy(tl_hbm, tl_ref, local_sems.at[3])
    load_ql.start()
    load_tl.start()
    load_q.start()
    load_t.start()
    load_ql.wait()
    load_tl.wait()
    ql_buf[0] = jnp.full((8, 128), ql_ref[c], jnp.int32)
    line = lax.broadcasted_iota(jnp.int32, (8, 128), 0)
    lengths = jnp.zeros((8, 128), jnp.int32)
    for r in range(per_core):
        lengths = jnp.where(line == r, tl_ref[r], lengths)
    tl_buf[0] = lengths
    pl.semaphore_wait(barrier, len(partners))

    split = res // 2
    halves = [pl.ds(0, split), pl.ds(split, split)]
    send_near = [
        remote(q_hbm.at[c, part], q_buf.at[1, part], q_sems, n, (near, grp))
        for n, part in enumerate(halves)
    ]
    pass_on = [
        remote(q_buf.at[1, part], q_buf.at[3, part], q_sems, 2 + n, (far, grp))
        for n, part in enumerate(halves)
    ]
    send_far = remote(q_hbm.at[c], q_buf.at[2], q_sems, 4, (far, grp))
    send_t = remote(t_hbm, t_buf.at[1], q_sems, 5, (blk, sibling))
    for copy in send_near:
        copy.start()
    send_t.start()
    send_len = [
        remote(ql_buf.at[0], ql_buf.at[s], l_sems, s - 1, (blks[s], grp)) for s in range(1, 4)
    ]
    send_len.append(remote(tl_buf.at[0], tl_buf.at[1], l_sems, 3, (blk, sibling)))
    for copy in send_len:
        copy.start()

    lane = lax.broadcasted_iota(jnp.int32, (8, 128), 1)
    col_at = lax.broadcasted_iota(jnp.int32, (res, res), 1)
    row_at = lax.broadcasted_iota(jnp.int32, (res, res), 0)

    def align(s, first, last):
        scores_all = lax.dot_general(
            q_buf[s],
            t_buf[first:last].reshape((last - first) * per_core * res, wide),
            (((1,), (1,)), ((), ())),
            preferred_element_type=jnp.float32,
        ) * scale
        row_ok_vec = (row_at < ql_buf[s, 0:1, :])[:, 0:1]
        for h, r in [(h, r) for h in range(first, last) for r in range(per_core)]:
            cols = slice(r * res, (r + 1) * res)
            at = ((h - first) * per_core + r) * res
            scores = scores_all[:, at : at + res]
            s_buf[s, h, :, cols] = scores
            by_row = jnp.where(col_at < tl_buf[h, r : r + 1, :], scores, LOW)
            row_exp = jnp.exp(by_row - jnp.max(by_row, axis=1, keepdims=True))
            row_inv = jnp.where(row_ok_vec, 1.0 / jnp.sum(row_exp, axis=1, keepdims=True), 0.0)
            row_soft = row_exp * row_inv
            w_buf[s, h, :, cols] = row_soft
            at = (h * per_core + r) * res
            a_buf[:, at : at + res] = row_soft.astype(jnp.bfloat16)

    def similar(s, h):
        row_ok = row_at < ql_buf[s, 0:1, :]
        place = ((blks[s] - blk + 4) % 4) * per_core
        tile = jnp.zeros((8, 128), jnp.float32)
        for r in range(per_core):
            cols = slice(r * res, (r + 1) * res)
            scores = s_buf[s, h, :, cols]
            row_soft = w_buf[s, h, :, cols]
            by_col = jnp.where(row_ok, scores, LOW)
            col_exp = jnp.exp(by_col - jnp.max(by_col, axis=0, keepdims=True))
            col_inv = jnp.where(
                col_at[0:1, :] < tl_buf[h, r : r + 1, :],
                1.0 / jnp.sum(col_exp, axis=0, keepdims=True),
                0.0,
            )
            col_soft = col_exp * col_inv
            weights = row_soft + col_soft - row_soft * col_soft
            upper = jnp.sum(
                jnp.sum(weights * scores, axis=0, keepdims=True), axis=1, keepdims=True
            )
            lower = jnp.sum(jnp.sum(weights, axis=0, keepdims=True), axis=1, keepdims=True)
            tile = jnp.where((line == c) & (lane == place + r), upper / lower, tile)
        tx_s[s, h] = tile

    def profile(s):
        r_buf[s] = jnp.dot(
            a_buf[...],
            t_buf[...].reshape(2 * per_core * res, wide),
            preferred_element_type=jnp.float32,
        )

    def both(s):
        align(s, 0, 2)
        profile(s)

    def similarities(s):
        def body(h, carry):
            similar(s, h)
            return carry

        lax.fori_loop(0, 2, body, 0)
        out = []
        for h in range(2):
            if s or h:
                copy = remote(
                    tx_s.at[s, h], rx_s.at[s, h], s_sems, s * 2 + h,
                    (blks[s], sibling if h else grp),
                )
                copy.start()
                out.append(copy)
        return out

    load_q.wait()
    load_t.wait()
    align(0, 0, 1)
    for n in range(2):
        send_near[n].wait_recv()
        pass_on[n].start()
    send_t.wait_recv()
    send_len[3].wait_recv()
    align(0, 1, 2)
    profile(0)
    send_far.start()

    send_len[0].wait_recv()
    both(1)
    encode(tx_a, slice(None), r_buf[1])
    send_a = remote(tx_a, rx_a, r_sems, 0, (near, grp))
    send_a.start()

    for n in range(2):
        pass_on[n].wait_recv()
    send_len[2].wait_recv()
    both(3)

    quarter = res // 4
    half = quarter // 2

    def chunk(i):
        return (z + 1 + i) % 4

    def rows(i):
        return pl.ds(pl.multiple_of(chunk(i) * quarter, quarter), quarter)

    send_b, send_c, send_z = [], [], []
    for i in range(4):
        encode(tx_b, rows(i), r_buf[3, rows(i), :])
        send_b.append(
            remote(tx_b.at[rows(i)], rx_b.at[rows(i)], r_sems, 1 + i, (near, grp))
        )
        send_b[i].start()

    send_far.wait_recv()
    send_len[1].wait_recv()
    both(2)

    def finish(i):
        if i == 0:
            send_a.wait_recv()
        send_c[i].wait_recv()
        summed = r_buf[0, rows(i), :] + decode(rx_a[rows(i), :]) + decode(rx_c[rows(i), :])
        encode(tx_z, rows(i), summed)
        if i == 3:
            r_buf[0, rows(i), :] = summed
        for u in range(2):
            core = 1 - c if u else c
            there = chunk(i) * 2 + core
            if i < 3 or u:
                mine = pl.ds(pl.multiple_of(there * half, half), half)
                copy = remote(
                    tx_z.at[mine], rx_z.at[i, u], z_sems, i * 2 + u, (blk, there)
                )
                copy.start()
                send_z.append(copy)

    for i in range(4):
        send_b[i].wait_recv()
        encode(tx_c, rows(i), r_buf[2, rows(i), :] + decode(rx_b[rows(i), :]))
        send_c.append(
            remote(tx_c.at[rows(i)], rx_c.at[rows(i)], r_sems, 5 + i, (far, grp))
        )
        send_c[i].start()
    sims = similarities(0)
    for i in range(4):
        finish(i)
    sims += similarities(1)
    sims += similarities(2)
    sims += similarities(3)

    total = tx_s[0, 0]
    for copy in sims:
        copy.wait_recv()
    for s in range(4):
        for h in range(2):
            if s or h:
                total = total + rx_s[s, h]
    sim_ref[...] = total[0:2, 0 : sim_ref.shape[1]]

    for copy in send_z:
        copy.wait_recv()
    own = pl.ds(pl.multiple_of(grp * half, half), half)
    prof_ref[c] = (
        r_buf[0, own, :] + decode(rx_z[0, 0]) + decode(rx_z[1, 0]) + decode(rx_z[2, 0])
    ) * profile_scale
    prof_ref[1 - c] = (
        decode(rx_z[0, 1]) + decode(rx_z[1, 1]) + decode(rx_z[2, 1]) + decode(rx_z[3, 1])
    ) * profile_scale

    for copy in (
        send_near + pass_on + [send_far, send_t, send_a]
        + send_len + sims + send_b + send_c + send_z
    ):
        copy.wait_send()


def plane_shards(queries, query_lengths, targets, target_lengths):
    sets, res, wide = queries.shape
    per_core = targets.shape[0]
    scale = 3.0 / math.sqrt(wide)
    profile_scale = 1.0 / math.sqrt(lax.axis_size("grp") * per_core * (STEPS + 1))
    part = res // lax.axis_size("grp")
    f32, bf16 = jnp.float32, jnp.bfloat16
    vmem = pltpu.VMEM
    return pl.pallas_call(
        functools.partial(kernel, scale, profile_scale),
        out_shape=(
            jax.ShapeDtypeStruct((sets, part, wide), f32),
            jax.ShapeDtypeStruct((sets, (STEPS + 1) * per_core), f32),
        ),
        in_specs=[
            pl.BlockSpec(memory_space=pltpu.HBM),
            pl.BlockSpec(memory_space=pltpu.HBM),
            pl.BlockSpec(memory_space=pltpu.HBM),
            pl.BlockSpec(memory_space=pltpu.HBM),
        ],
        out_specs=(pl.BlockSpec(memory_space=vmem), pl.BlockSpec(memory_space=vmem)),
        scratch_shapes=[
            vmem((4, res, wide), bf16),
            vmem((2, per_core, res, wide), bf16),
            vmem((4, 8, 128), jnp.int32),
            vmem((2, 8, 128), jnp.int32),
            vmem((4, 2, res, per_core * res), f32),
            vmem((4, 2, res, per_core * res), f32),
            vmem((res, 2 * per_core * res), bf16),
            vmem((4, res, wide), f32),
            *[vmem((res, wide + 128), jnp.int16) for _ in range(7)],
            vmem((4, 2, part, wide + 128), jnp.int16),
            vmem((4, 2, 8, 128), f32),
            vmem((4, 2, 8, 128), f32),
            pltpu.SMEM(query_lengths.shape, jnp.int32),
            pltpu.SMEM(target_lengths.shape, jnp.int32),
            pltpu.SemaphoreType.DMA((4,)),
            pltpu.SemaphoreType.DMA((2, 6)),
            pltpu.SemaphoreType.DMA((2, 4)),
            pltpu.SemaphoreType.DMA((2, 9)),
            pltpu.SemaphoreType.DMA((2, 8)),
            pltpu.SemaphoreType.DMA((2, 8)),
        ],
        compiler_params=pltpu.CompilerParams(
            collective_id=0, has_side_effects=True, vmem_limit_bytes=56 * 1024 * 1024
        ),
    )(query_lengths, target_lengths, queries, targets)


def solution(mesh):
    in_specs = (P("blk", None, None), P("blk"), P(("blk", "grp"), None, None), P(("blk", "grp")))
    out_specs = (P("blk", "grp", None), P("blk", "grp"))
    plane = mesh.shape["blk"] == STEPS + 1 == 4 and mesh.shape["grp"] == 8
    shards = plane_shards if plane else ring_shards
    return jax.shard_map(shards, mesh=mesh, in_specs=in_specs, out_specs=out_specs, check_vma=False)
```

```python
import functools
import math

import jax
import jax.numpy as jnp
from jax import lax
from jax.experimental import pallas as pl
from jax.experimental.pallas import tpu as pltpu
from jax.sharding import PartitionSpec as P

STEPS = 3
MESH = pl.DeviceIdType.MESH
LOW = -1e30
CODES = 32000.0


def from_behind(array, axis, by):
    length = lax.axis_size(axis)
    return lax.ppermute(array, axis, [(i, (i + by) % length) for i in range(length)])


def align_pair(query_rows, query_len, target_rows, target_len):
    scale = 3.0 / math.sqrt(query_rows.shape[-1])
    scores = (
        jnp.einsum("qid,mjd->qmij", query_rows, target_rows, preferred_element_type=jnp.float32)
        * scale
    )
    positions = lax.broadcasted_iota(jnp.float32, (1, query_rows.shape[1]), 1)
    row_ok = positions < query_len[:, None]
    col_ok = positions < target_len[:, None]
    row_mask = row_ok[:, None, :, None]
    col_mask = col_ok[None, :, None, :]
    row_top = jnp.max(jnp.where(col_mask, scores, -jnp.inf), axis=3, keepdims=True)
    row_exp = jnp.where(col_mask, jnp.exp(scores - row_top), 0.0)
    row_soft = jnp.where(row_mask, row_exp / jnp.sum(row_exp, axis=3, keepdims=True), 0.0)
    col_top = jnp.max(jnp.where(row_mask, scores, -jnp.inf), axis=2, keepdims=True)
    col_exp = jnp.where(row_mask, jnp.exp(scores - col_top), 0.0)
    col_soft = jnp.where(col_mask, col_exp / jnp.sum(col_exp, axis=2, keepdims=True), 0.0)
    weights = row_soft + col_soft - row_soft * col_soft
    similarity = jnp.sum(weights * scores, axis=(2, 3)) / jnp.sum(weights, axis=(2, 3))
    profile = jnp.einsum(
        "qmij,mjd->qid",
        row_soft.astype(jnp.bfloat16),
        target_rows,
        preferred_element_type=jnp.float32,
    )
    return (similarity, profile)


def ring_shards(queries, query_lengths, targets, target_lengths):
    blocks = targets.shape[0]
    group_size = lax.axis_size("grp")
    profile_scale = 1.0 / math.sqrt(group_size * blocks * (STEPS + 1))
    resident = (targets, target_lengths.astype(jnp.bfloat16))
    running = jnp.zeros(queries.shape, jnp.float32)
    arrived = [resident] + [
        from_behind((resident[0], resident[1]), "blk", offset) for offset in range(1, STEPS + 1)
    ]
    query_len = query_lengths.astype(jnp.float32)
    collected = []
    for visiting in arrived:
        pair_sim, pair_prof = align_pair(
            queries, query_len, visiting[0], visiting[1].astype(jnp.float32)
        )
        running = running + pair_prof
        collected.append(pair_sim)
    similarity = jnp.concatenate(collected, axis=1)
    shares = lax.psum_scatter(running, "grp", scatter_dimension=1, tiled=True) * profile_scale
    return (shares, similarity)


def remote(src, dst, sems, k, device):
    return pltpu.make_async_remote_copy(
        src_ref=src,
        dst_ref=dst,
        send_sem=sems.at[0, k],
        recv_sem=sems.at[1, k],
        device_id=device,
        device_id_type=MESH,
    )


def encode(dst, at, values):
    wide = values.shape[1]
    top = jnp.maximum(jnp.max(jnp.abs(values), axis=1, keepdims=True), 2.0**-110)
    power = jnp.ceil(jnp.log2(top) * 64.0)
    factor = jnp.exp2(power * (-1.0 / 64.0)) * CODES
    dst[at, 0:wide] = jnp.round(values * factor).astype(jnp.int32).astype(jnp.int16)
    dst[at, wide:] = (
        jnp.broadcast_to(power, (values.shape[0], 128)).astype(jnp.int32).astype(jnp.int16)
    )


def decode(coded):
    wide = coded.shape[1] - 128
    power = coded[:, wide:].astype(jnp.int32).astype(jnp.float32)
    factor = jnp.exp2(power * (1.0 / 64.0)) * (1.0 / CODES)
    values = coded[:, 0:wide].astype(jnp.int32).astype(jnp.float32)
    return values * jnp.concatenate([factor] * (wide // 128), axis=1)


def kernel(
    scale, profile_scale,
    ql_hbm, tl_hbm, q_hbm, t_hbm, prof_ref, sim_ref,
    q_buf, t_buf, ql_buf, tl_buf, s_buf, w_buf, a_buf, r_buf, tx, rx, rx_z,
    tx_s, rx_s, ql_ref, tl_ref,
    local_sems, q_sems, l_sems, r_sems, z_sems, s_sems,
):
    res, wide = q_buf.shape[1:]
    per_core = t_buf.shape[1]
    blk, grp = lax.axis_index("blk"), lax.axis_index("grp")
    x, y = blk % 2, blk // 2
    c, z = grp % 2, grp // 2
    other_x, other_y = y * 2 + (1 - x), (1 - y) * 2 + x
    near = other_x * (1 - c) + other_y * c
    far = other_y * (1 - c) + other_x * c
    blks = (blk, near, 3 - blk, far)
    sibling = z * 2 + (1 - c)

    barrier = pltpu.get_barrier_semaphore()
    partners = [(b, grp) for b in blks[1:]] + [(b, sibling) for b in blks]
    for step in range(1, 4):
        there = (z + step) % 4
        partners += [(blk, there * 2 + c), (blk, there * 2 + (1 - c))]
    for partner in partners:
        pl.semaphore_signal(barrier, inc=1, device_id=partner, device_id_type=MESH)

    load_q = pltpu.make_async_copy(q_hbm.at[c], q_buf.at[0], local_sems.at[0])
    load_t = pltpu.make_async_copy(t_hbm, t_buf.at[0], local_sems.at[1])
    load_ql = pltpu.make_async_copy(ql_hbm, ql_ref, local_sems.at[2])
    load_tl = pltpu.make_async_copy(tl_hbm, tl_ref, local_sems.at[3])
    load_ql.start()
    load_tl.start()
    load_q.start()
    load_t.start()
    load_ql.wait()
    load_tl.wait()
    ql_buf[0] = jnp.full((8, 128), ql_ref[c], jnp.int32)
    line = lax.broadcasted_iota(jnp.int32, (8, 128), 0)
    lengths = jnp.zeros((8, 128), jnp.int32)
    for r in range(per_core):
        lengths = jnp.where(line == r, tl_ref[r], lengths)
    tl_buf[0] = lengths
    pl.semaphore_wait(barrier, len(partners))

    split = res // 2
    halves = [pl.ds(0, split), pl.ds(split, split)]
    send_near = [
        remote(q_hbm.at[c, part], q_buf.at[1, part], q_sems, n, (near, grp))
        for n, part in enumerate(halves)
    ]
    pass_on = [
        remote(q_buf.at[1, part], q_buf.at[2, part], q_sems, 2 + n, (far, grp))
        for n, part in enumerate(halves)
    ]
    send_far = remote(q_hbm.at[c], q_buf.at[3], q_sems, 4, (far, grp))
    send_t = remote(t_hbm, t_buf.at[1], q_sems, 5, (blk, sibling))
    for copy in send_near:
        copy.start()
    send_t.start()
    send_len = [
        remote(ql_buf.at[0], ql_buf.at[s], l_sems, s - 1, (blks[s], grp)) for s in range(1, 4)
    ]
    send_len.append(remote(tl_buf.at[0], tl_buf.at[1], l_sems, 3, (blk, sibling)))
    for copy in send_len:
        copy.start()

    lane = lax.broadcasted_iota(jnp.int32, (8, 128), 1)
    col_at = lax.broadcasted_iota(jnp.int32, (res, res), 1)
    row_at = lax.broadcasted_iota(jnp.int32, (res, res), 0)
    quarter = res // 4
    half = quarter // 2

    def chunk(i):
        return (z + 1 + i) % 4

    def rows(i):
        return pl.ds(pl.multiple_of(chunk(i) * quarter, quarter), quarter)

    def sum_copy(s, i):
        return remote(tx.at[s, rows(i)], rx.at[s, rows(i)], r_sems, s * 4 + i, (near, grp))

    def far_copy(i):
        return remote(tx.at[2, rows(i)], rx.at[2, rows(i)], r_sems, 8 + i, (far, grp))

    def z_copy(i, u):
        there = chunk(i) * 2 + (1 - c if u else c)
        mine = pl.ds(pl.multiple_of(there * half, half), half)
        return remote(tx.at[3, mine], rx_z.at[i, u], z_sems, i * 2 + u, (blk, there))

    def align(s, h):
        scores_all = lax.dot_general(
            q_buf[s],
            t_buf[h].reshape(per_core * res, wide),
            (((1,), (1,)), ((), ())),
            preferred_element_type=jnp.float32,
        ) * scale
        row_ok_vec = (row_at < ql_buf[s, 0:1, :])[:, 0:1]
        for r in range(per_core):
            cols = slice(r * res, (r + 1) * res)
            scores = scores_all[:, cols]
            s_buf[s, h, :, cols] = scores
            by_row = jnp.where(col_at < tl_buf[h, r : r + 1, :], scores, LOW)
            row_exp = jnp.exp(by_row - jnp.max(by_row, axis=1, keepdims=True))
            row_inv = jnp.where(row_ok_vec, 1.0 / jnp.sum(row_exp, axis=1, keepdims=True), 0.0)
            row_soft = row_exp * row_inv
            w_buf[s, h, :, cols] = row_soft
            a_buf[h, :, cols] = row_soft.astype(jnp.bfloat16)

    def profile(s):
        r_buf[s] = sum(
            jnp.dot(
                a_buf[h],
                t_buf[h].reshape(per_core * res, wide),
                preferred_element_type=jnp.float32,
            )
            for h in range(2)
        )

    def similar(s, h):
        row_ok = row_at < ql_buf[s, 0:1, :]
        peer = (
            blk
            + (s * (3 - s) * (2 - s) // 2) * (near - blk)
            + (s * (3 - s) * (s - 1) // 2) * (3 - 2 * blk)
            + (s * (s - 1) * (s - 2) // 6) * (far - blk)
        )
        place = ((peer - blk + 4) % 4) * per_core
        tile = jnp.zeros((8, 128), jnp.float32)
        for r in range(per_core):
            cols = slice(r * res, (r + 1) * res)
            scores = s_buf[s, h, :, cols]
            row_soft = w_buf[s, h, :, cols]
            by_col = jnp.where(row_ok, scores, LOW)
            col_exp = jnp.exp(by_col - jnp.max(by_col, axis=0, keepdims=True))
            col_inv = jnp.where(
                col_at[0:1, :] < tl_buf[h, pl.ds(r, 1), :],
                1.0 / jnp.sum(col_exp, axis=0, keepdims=True),
                0.0,
            )
            col_soft = col_exp * col_inv
            weights = row_soft + col_soft - row_soft * col_soft
            upper = jnp.sum(
                jnp.sum(weights * scores, axis=0, keepdims=True), axis=1, keepdims=True
            )
            lower = jnp.sum(jnp.sum(weights, axis=0, keepdims=True), axis=1, keepdims=True)
            tile = jnp.where((line == c) & (lane == place + r), upper / lower, tile)
        tx_s[s, h] = tile

    load_q.wait()
    load_t.wait()

    @pl.loop(0, 8)
    def _(n):
        s, h = n // 2, n % 2

        @pl.when(n == 1)
        def _():
            for m in range(2):
                send_near[m].wait_recv()
                pass_on[m].start()
            send_t.wait_recv()
            send_len[3].wait_recv()

        @pl.when(n == 2)
        def _():
            send_far.start()
            send_len[0].wait_recv()

        @pl.when(n == 4)
        def _():
            for m in range(2):
                pass_on[m].wait_recv()
            send_len[1].wait_recv()

        @pl.when(n == 6)
        def _():
            send_far.wait_recv()
            send_len[2].wait_recv()

        align(s, h)

        @pl.when(h == 1)
        def _():
            profile(s)

        @pl.when((n == 3) | (n == 5))
        def _():
            @pl.loop(0, 4)
            def _(i):
                encode(tx.at[s - 1], rows(i), r_buf[s, rows(i), :])
                sum_copy(s - 1, i).start()

    @pl.loop(0, 4)
    def _(i):
        sum_copy(1, i).wait_recv()
        encode(tx.at[2], rows(i), r_buf[3, rows(i), :] + decode(rx[1, rows(i), :]))
        far_copy(i).start()

    @pl.loop(0, 4)
    def _(i):
        sum_copy(0, i).wait_recv()
        far_copy(i).wait_recv()
        summed = r_buf[0, rows(i), :] + decode(rx[0, rows(i), :]) + decode(rx[2, rows(i), :])
        r_buf[0, rows(i), :] = summed
        encode(tx.at[3], rows(i), summed)
        z_copy(i, 1).start()

        @pl.when(i < 3)
        def _():
            z_copy(i, 0).start()

    @pl.loop(0, 8)
    def _(n):
        similar(n // 2, n % 2)

    sims = [
        remote(
            tx_s.at[s, h], rx_s.at[s, h], s_sems, s * 2 + h, (blks[s], sibling if h else grp)
        )
        for s in range(4) for h in range(2) if s or h
    ]
    for copy in sims:
        copy.start()

    own = pl.ds(pl.multiple_of(grp * half, half), half)
    here, there = r_buf[0, own, :], None
    for i in range(4):
        z_copy(i, 1).wait_recv()
        part = decode(rx_z[i, 1])
        there = part if there is None else there + part
        if i < 3:
            z_copy(i, 0).wait_recv()
            here = here + decode(rx_z[i, 0])
    prof_ref[c] = here * profile_scale
    prof_ref[1 - c] = there * profile_scale

    total = tx_s[0, 0]
    for copy in sims:
        copy.wait_recv()
    for s in range(4):
        for h in range(2):
            if s or h:
                total = total + rx_s[s, h]
    sim_ref[...] = total[0:2, 0 : sim_ref.shape[1]]

    for copy in send_near + pass_on + [send_far, send_t] + send_len + sims:
        copy.wait_send()
    for i in range(4):
        sum_copy(0, i).wait_send()
        sum_copy(1, i).wait_send()
        far_copy(i).wait_send()
        z_copy(i, 1).wait_send()
        if i < 3:
            z_copy(i, 0).wait_send()


def plane_shards(queries, query_lengths, targets, target_lengths):
    sets, res, wide = queries.shape
    per_core = targets.shape[0]
    scale = 3.0 / math.sqrt(wide)
    profile_scale = 1.0 / math.sqrt(lax.axis_size("grp") * per_core * (STEPS + 1))
    part = res // lax.axis_size("grp")
    f32, bf16 = jnp.float32, jnp.bfloat16
    vmem = pltpu.VMEM
    return pl.pallas_call(
        functools.partial(kernel, scale, profile_scale),
        out_shape=(
            jax.ShapeDtypeStruct((sets, part, wide), f32),
            jax.ShapeDtypeStruct((sets, (STEPS + 1) * per_core), f32),
        ),
        in_specs=[
            pl.BlockSpec(memory_space=pltpu.HBM),
            pl.BlockSpec(memory_space=pltpu.HBM),
            pl.BlockSpec(memory_space=pltpu.HBM),
            pl.BlockSpec(memory_space=pltpu.HBM),
        ],
        out_specs=(pl.BlockSpec(memory_space=vmem), pl.BlockSpec(memory_space=vmem)),
        scratch_shapes=[
            vmem((4, res, wide), bf16),
            vmem((2, per_core, res, wide), bf16),
            vmem((4, 8, 128), jnp.int32),
            vmem((2, 8, 128), jnp.int32),
            vmem((4, 2, res, per_core * res), f32),
            vmem((4, 2, res, per_core * res), f32),
            vmem((2, res, per_core * res), bf16),
            vmem((4, res, wide), f32),
            vmem((4, res, wide + 128), jnp.int16),
            vmem((3, res, wide + 128), jnp.int16),
            vmem((4, 2, part, wide + 128), jnp.int16),
            vmem((4, 2, 8, 128), f32),
            vmem((4, 2, 8, 128), f32),
            pltpu.SMEM(query_lengths.shape, jnp.int32),
            pltpu.SMEM(target_lengths.shape, jnp.int32),
            pltpu.SemaphoreType.DMA((4,)),
            pltpu.SemaphoreType.DMA((2, 6)),
            pltpu.SemaphoreType.DMA((2, 4)),
            pltpu.SemaphoreType.DMA((2, 12)),
            pltpu.SemaphoreType.DMA((2, 8)),
            pltpu.SemaphoreType.DMA((2, 8)),
        ],
        compiler_params=pltpu.CompilerParams(
            collective_id=0, has_side_effects=True, vmem_limit_bytes=56 * 1024 * 1024
        ),
    )(query_lengths, target_lengths, queries, targets)


def solution(mesh):
    in_specs = (P("blk", None, None), P("blk"), P(("blk", "grp"), None, None), P(("blk", "grp")))
    out_specs = (P("blk", "grp", None), P("blk", "grp"))
    plane = mesh.shape["blk"] == STEPS + 1 == 4 and mesh.shape["grp"] == 8
    shards = plane_shards if plane else ring_shards
    return jax.shard_map(shards, mesh=mesh, in_specs=in_specs, out_specs=out_specs, check_vma=False)
```

```python
import functools
import math

import jax
import jax.numpy as jnp
from jax import lax
from jax.experimental import pallas as pl
from jax.experimental.pallas import tpu as pltpu
from jax.sharding import PartitionSpec as P

STEPS = 3
MESH = pl.DeviceIdType.MESH
LOW = -1e30
CODES = 32000.0


def from_behind(array, axis, by):
    length = lax.axis_size(axis)
    return lax.ppermute(array, axis, [(i, (i + by) % length) for i in range(length)])


def align_pair(query_rows, query_len, target_rows, target_len):
    scale = 3.0 / math.sqrt(query_rows.shape[-1])
    scores = (
        jnp.einsum("qid,mjd->qmij", query_rows, target_rows, preferred_element_type=jnp.float32)
        * scale
    )
    positions = lax.broadcasted_iota(jnp.float32, (1, query_rows.shape[1]), 1)
    row_ok = positions < query_len[:, None]
    col_ok = positions < target_len[:, None]
    row_mask = row_ok[:, None, :, None]
    col_mask = col_ok[None, :, None, :]
    row_top = jnp.max(jnp.where(col_mask, scores, -jnp.inf), axis=3, keepdims=True)
    row_exp = jnp.where(col_mask, jnp.exp(scores - row_top), 0.0)
    row_soft = jnp.where(row_mask, row_exp / jnp.sum(row_exp, axis=3, keepdims=True), 0.0)
    col_top = jnp.max(jnp.where(row_mask, scores, -jnp.inf), axis=2, keepdims=True)
    col_exp = jnp.where(row_mask, jnp.exp(scores - col_top), 0.0)
    col_soft = jnp.where(col_mask, col_exp / jnp.sum(col_exp, axis=2, keepdims=True), 0.0)
    weights = row_soft + col_soft - row_soft * col_soft
    similarity = jnp.sum(weights * scores, axis=(2, 3)) / jnp.sum(weights, axis=(2, 3))
    profile = jnp.einsum(
        "qmij,mjd->qid",
        row_soft.astype(jnp.bfloat16),
        target_rows,
        preferred_element_type=jnp.float32,
    )
    return (similarity, profile)


def ring_shards(queries, query_lengths, targets, target_lengths):
    blocks = targets.shape[0]
    group_size = lax.axis_size("grp")
    profile_scale = 1.0 / math.sqrt(group_size * blocks * (STEPS + 1))
    resident = (targets, target_lengths.astype(jnp.bfloat16))
    running = jnp.zeros(queries.shape, jnp.float32)
    arrived = [resident] + [
        from_behind((resident[0], resident[1]), "blk", offset) for offset in range(1, STEPS + 1)
    ]
    query_len = query_lengths.astype(jnp.float32)
    collected = []
    for visiting in arrived:
        pair_sim, pair_prof = align_pair(
            queries, query_len, visiting[0], visiting[1].astype(jnp.float32)
        )
        running = running + pair_prof
        collected.append(pair_sim)
    similarity = jnp.concatenate(collected, axis=1)
    shares = lax.psum_scatter(running, "grp", scatter_dimension=1, tiled=True) * profile_scale
    return (shares, similarity)


def remote(src, dst, sems, k, device):
    return pltpu.make_async_remote_copy(
        src_ref=src,
        dst_ref=dst,
        send_sem=sems.at[0, k],
        recv_sem=sems.at[1, k],
        device_id=device,
        device_id_type=MESH,
    )


def encode(dst, at, values):
    wide = values.shape[1]
    top = jnp.maximum(jnp.max(jnp.abs(values), axis=1, keepdims=True), 2.0**-110)
    power = jnp.ceil(jnp.log2(top) * 64.0)
    factor = jnp.exp2(power * (-1.0 / 64.0)) * CODES
    dst[at, 0:wide] = jnp.round(values * factor).astype(jnp.int32).astype(jnp.int16)
    dst[at, wide:] = (
        jnp.broadcast_to(power, (values.shape[0], 128)).astype(jnp.int32).astype(jnp.int16)
    )


def decode(coded):
    wide = coded.shape[1] - 128
    power = coded[:, wide:].astype(jnp.int32).astype(jnp.float32)
    factor = jnp.exp2(power * (1.0 / 64.0)) * (1.0 / CODES)
    values = coded[:, 0:wide].astype(jnp.int32).astype(jnp.float32)
    return values * jnp.concatenate([factor] * (wide // 128), axis=1)


def kernel(
    scale, profile_scale,
    ql_hbm, tl_hbm, q_hbm, t_hbm, prof_ref, sim_ref,
    q_buf, t_buf, ql_buf, tl_buf, s_buf, w_buf, a_buf, r_buf, tx_a, tx_b, tx_c, tx_z, rx_a, rx_b, rx_c, rx_z,
    tx_s, rx_s, ql_ref, tl_ref,
    local_sems, q_sems, l_sems, r_sems, z_sems, s_sems,
):
    res, wide = q_buf.shape[1:]
    per_core = t_buf.shape[1]
    blk, grp = lax.axis_index("blk"), lax.axis_index("grp")
    x, y = blk % 2, blk // 2
    c, z = grp % 2, grp // 2
    other_x, other_y = y * 2 + (1 - x), (1 - y) * 2 + x
    near = other_x * (1 - c) + other_y * c
    far = other_y * (1 - c) + other_x * c
    blks = (blk, near, far, 3 - blk)
    sibling = z * 2 + (1 - c)

    barrier = pltpu.get_barrier_semaphore()
    partners = [(b, grp) for b in blks[1:]] + [(b, sibling) for b in blks]
    for step in range(1, 4):
        there = (z + step) % 4
        partners += [(blk, there * 2 + c), (blk, there * 2 + (1 - c))]
    for partner in partners:
        pl.semaphore_signal(barrier, inc=1, device_id=partner, device_id_type=MESH)

    load_q = pltpu.make_async_copy(q_hbm.at[c], q_buf.at[0], local_sems.at[0])
    load_t = pltpu.make_async_copy(t_hbm, t_buf.at[0], local_sems.at[1])
    load_ql = pltpu.make_async_copy(ql_hbm, ql_ref, local_sems.at[2])
    load_tl = pltpu.make_async_copy(tl_hbm, tl_ref, local_sems.at[3])
    load_ql.start()
    load_tl.start()
    load_q.start()
    load_t.start()
    load_ql.wait()
    load_tl.wait()
    ql_buf[0] = jnp.full((8, 128), ql_ref[c], jnp.int32)
    line = lax.broadcasted_iota(jnp.int32, (8, 128), 0)
    lengths = jnp.zeros((8, 128), jnp.int32)
    for r in range(per_core):
        lengths = jnp.where(line == r, tl_ref[r], lengths)
    tl_buf[0] = lengths
    pl.semaphore_wait(barrier, len(partners))

    split = res // 2
    halves = [pl.ds(0, split), pl.ds(split, split)]
    send_near = [
        remote(q_hbm.at[c, part], q_buf.at[1, part], q_sems, n, (near, grp))
        for n, part in enumerate(halves)
    ]
    pass_on = [
        remote(q_buf.at[1, part], q_buf.at[3, part], q_sems, 2 + n, (far, grp))
        for n, part in enumerate(halves)
    ]
    send_far = remote(q_hbm.at[c], q_buf.at[2], q_sems, 4, (far, grp))
    send_t = remote(t_hbm, t_buf.at[1], q_sems, 5, (blk, sibling))
    for copy in send_near:
        copy.start()
    send_t.start()
    send_len = [
        remote(ql_buf.at[0], ql_buf.at[s], l_sems, s - 1, (blks[s], grp)) for s in range(1, 4)
    ]
    send_len.append(remote(tl_buf.at[0], tl_buf.at[1], l_sems, 3, (blk, sibling)))
    for copy in send_len:
        copy.start()

    lane = lax.broadcasted_iota(jnp.int32, (8, 128), 1)
    col_at = lax.broadcasted_iota(jnp.int32, (res, res), 1)
    row_at = lax.broadcasted_iota(jnp.int32, (res, res), 0)

    def align(s, first, last):
        scores_all = lax.dot_general(
            q_buf[s],
            t_buf[first:last].reshape((last - first) * per_core * res, wide),
            (((1,), (1,)), ((), ())),
            preferred_element_type=jnp.float32,
        ) * scale
        row_ok_vec = (row_at < ql_buf[s, 0:1, :])[:, 0:1]
        for h, r in [(h, r) for h in range(first, last) for r in range(per_core)]:
            cols = slice(r * res, (r + 1) * res)
            at = ((h - first) * per_core + r) * res
            scores = scores_all[:, at : at + res]
            s_buf[s, h, :, cols] = scores
            by_row = jnp.where(col_at < tl_buf[h, r : r + 1, :], scores, LOW)
            row_exp = jnp.exp(by_row - jnp.max(by_row, axis=1, keepdims=True))
            row_inv = jnp.where(row_ok_vec, 1.0 / jnp.sum(row_exp, axis=1, keepdims=True), 0.0)
            row_soft = row_exp * row_inv
            w_buf[s, h, :, cols] = row_soft
            at = (h * per_core + r) * res
            a_buf[:, at : at + res] = row_soft.astype(jnp.bfloat16)

    def similar(s, h):
        row_ok = row_at < ql_buf[s, 0:1, :]
        place = ((blks[s] - blk + 4) % 4) * per_core
        tile = jnp.zeros((8, 128), jnp.float32)
        for r in range(per_core):
            cols = slice(r * res, (r + 1) * res)
            scores = s_buf[s, h, :, cols]
            row_soft = w_buf[s, h, :, cols]
            by_col = jnp.where(row_ok, scores, LOW)
            col_exp = jnp.exp(by_col - jnp.max(by_col, axis=0, keepdims=True))
            col_inv = jnp.where(
                col_at[0:1, :] < tl_buf[h, r : r + 1, :],
                1.0 / jnp.sum(col_exp, axis=0, keepdims=True),
                0.0,
            )
            col_soft = col_exp * col_inv
            weights = row_soft + col_soft - row_soft * col_soft
            upper = jnp.sum(
                jnp.sum(weights * scores, axis=0, keepdims=True), axis=1, keepdims=True
            )
            lower = jnp.sum(jnp.sum(weights, axis=0, keepdims=True), axis=1, keepdims=True)
            tile = jnp.where((line == c) & (lane == place + r), upper / lower, tile)
        tx_s[s, h] = tile

    def profile(s):
        r_buf[s] = jnp.dot(
            a_buf[...],
            t_buf[...].reshape(2 * per_core * res, wide),
            preferred_element_type=jnp.float32,
        )

    def both(s):
        align(s, 0, 2)
        profile(s)

    def similarities(s):
        def body(h, carry):
            similar(s, h)
            return carry

        lax.fori_loop(0, 2, body, 0)
        out = []
        for h in range(2):
            if s or h:
                copy = remote(
                    tx_s.at[s, h], rx_s.at[s, h], s_sems, s * 2 + h,
                    (blks[s], sibling if h else grp),
                )
                copy.start()
                out.append(copy)
        return out

    load_q.wait()
    load_t.wait()
    align(0, 0, 1)
    for n in range(2):
        send_near[n].wait_recv()
        pass_on[n].start()
    send_t.wait_recv()
    send_len[3].wait_recv()
    align(0, 1, 2)
    profile(0)
    send_far.start()

    send_len[0].wait_recv()
    both(1)
    encode(tx_a, slice(None), r_buf[1])
    send_a = remote(tx_a, rx_a, r_sems, 0, (near, grp))
    send_a.start()

    for n in range(2):
        pass_on[n].wait_recv()
    send_len[2].wait_recv()
    both(3)

    quarter = res // 4
    half = quarter // 2

    def chunk(i):
        return (z + 1 + i) % 4

    def rows(i):
        return pl.ds(pl.multiple_of(chunk(i) * quarter, quarter), quarter)

    send_b, send_c, send_z = [], [], []
    for i in range(4):
        encode(tx_b, rows(i), r_buf[3, rows(i), :])
        send_b.append(
            remote(tx_b.at[rows(i)], rx_b.at[rows(i)], r_sems, 1 + i, (near, grp))
        )
        send_b[i].start()

    send_far.wait_recv()
    send_len[1].wait_recv()
    both(2)

    def finish(i):
        if i == 0:
            send_a.wait_recv()
        send_c[i].wait_recv()
        summed = r_buf[0, rows(i), :] + decode(rx_a[rows(i), :]) + decode(rx_c[rows(i), :])
        encode(tx_z, rows(i), summed)
        if i == 3:
            r_buf[0, rows(i), :] = summed
        for u in range(2):
            core = 1 - c if u else c
            there = chunk(i) * 2 + core
            if i < 3 or u:
                mine = pl.ds(pl.multiple_of(there * half, half), half)
                copy = remote(
                    tx_z.at[mine], rx_z.at[i, u], z_sems, i * 2 + u, (blk, there)
                )
                copy.start()
                send_z.append(copy)

    for i in range(4):
        send_b[i].wait_recv()
        encode(tx_c, rows(i), r_buf[2, rows(i), :] + decode(rx_b[rows(i), :]))
        send_c.append(
            remote(tx_c.at[rows(i)], rx_c.at[rows(i)], r_sems, 5 + i, (far, grp))
        )
        send_c[i].start()
    for i in range(4):
        finish(i)
    sims = similarities(0)
    sims += similarities(1)
    sims += similarities(2)
    sims += similarities(3)

    total = tx_s[0, 0]
    for copy in sims:
        copy.wait_recv()
    for s in range(4):
        for h in range(2):
            if s or h:
                total = total + rx_s[s, h]
    sim_ref[...] = total[0:2, 0 : sim_ref.shape[1]]

    for copy in send_z:
        copy.wait_recv()
    own = pl.ds(pl.multiple_of(grp * half, half), half)
    prof_ref[c] = (
        r_buf[0, own, :] + decode(rx_z[0, 0]) + decode(rx_z[1, 0]) + decode(rx_z[2, 0])
    ) * profile_scale
    prof_ref[1 - c] = (
        decode(rx_z[0, 1]) + decode(rx_z[1, 1]) + decode(rx_z[2, 1]) + decode(rx_z[3, 1])
    ) * profile_scale

    for copy in (
        send_near + pass_on + [send_far, send_t, send_a]
        + send_len + sims + send_b + send_c + send_z
    ):
        copy.wait_send()


def plane_shards(queries, query_lengths, targets, target_lengths):
    sets, res, wide = queries.shape
    per_core = targets.shape[0]
    scale = 3.0 / math.sqrt(wide)
    profile_scale = 1.0 / math.sqrt(lax.axis_size("grp") * per_core * (STEPS + 1))
    part = res // lax.axis_size("grp")
    f32, bf16 = jnp.float32, jnp.bfloat16
    vmem = pltpu.VMEM
    return pl.pallas_call(
        functools.partial(kernel, scale, profile_scale),
        out_shape=(
            jax.ShapeDtypeStruct((sets, part, wide), f32),
            jax.ShapeDtypeStruct((sets, (STEPS + 1) * per_core), f32),
        ),
        in_specs=[
            pl.BlockSpec(memory_space=pltpu.HBM),
            pl.BlockSpec(memory_space=pltpu.HBM),
            pl.BlockSpec(memory_space=pltpu.HBM),
            pl.BlockSpec(memory_space=pltpu.HBM),
        ],
        out_specs=(pl.BlockSpec(memory_space=vmem), pl.BlockSpec(memory_space=vmem)),
        scratch_shapes=[
            vmem((4, res, wide), bf16),
            vmem((2, per_core, res, wide), bf16),
            vmem((4, 8, 128), jnp.int32),
            vmem((2, 8, 128), jnp.int32),
            vmem((4, 2, res, per_core * res), f32),
            vmem((4, 2, res, per_core * res), f32),
            vmem((res, 2 * per_core * res), bf16),
            vmem((4, res, wide), f32),
            *[vmem((res, wide + 128), jnp.int16) for _ in range(7)],
            vmem((4, 2, part, wide + 128), jnp.int16),
            vmem((4, 2, 8, 128), f32),
            vmem((4, 2, 8, 128), f32),
            pltpu.SMEM(query_lengths.shape, jnp.int32),
            pltpu.SMEM(target_lengths.shape, jnp.int32),
            pltpu.SemaphoreType.DMA((4,)),
            pltpu.SemaphoreType.DMA((2, 6)),
            pltpu.SemaphoreType.DMA((2, 4)),
            pltpu.SemaphoreType.DMA((2, 9)),
            pltpu.SemaphoreType.DMA((2, 8)),
            pltpu.SemaphoreType.DMA((2, 8)),
        ],
        compiler_params=pltpu.CompilerParams(
            collective_id=0, has_side_effects=True, vmem_limit_bytes=56 * 1024 * 1024
        ),
    )(query_lengths, target_lengths, queries, targets)


def solution(mesh):
    in_specs = (P("blk", None, None), P("blk"), P(("blk", "grp"), None, None), P(("blk", "grp")))
    out_specs = (P("blk", "grp", None), P("blk", "grp"))
    plane = mesh.shape["blk"] == STEPS + 1 == 4 and mesh.shape["grp"] == 8
    shards = plane_shards if plane else ring_shards
    return jax.shard_map(shards, mesh=mesh, in_specs=in_specs, out_specs=out_specs, check_vma=False)
```
